128 devices in a mesh: dp: 8 (over y, core), vocab: 16 (over x, z).
Axes of the slice: x: 4, y: 4, z: 4, core: 2. Of those that a mesh axis runs over, the one named last changes fastest.
Arguments:
- latent_vectors: bfloat16 [1024, 7168], P('dp'), may hold values from -80 to 80
- unembedding_matrix: bfloat16 [7168, 129280], P(None, ('dp', 'vocab')), may hold values from -0.19921875 to 0.19921875
- softmax_divisor: float32 [1024], P('dp'), may hold values from 0.5 to 1.5
- top_probability_quota: int32 [1024], P('dp'), may hold values from 50 to 99
Outputs:
- nucleus: float32 [1024, 129280], P(None, ('dp', 'vocab'))
The draws below stay inside these ranges and needn't reach their ends.
All inputs are finite; a program needn't handle non-finite values.
Results may differ from the reference program's by a relative error of at most 0.00185.
Values may be sent and summed in bfloat16 or wider, within the bound.
A program may use at most 128 MiB of HBM per device.

```python
import math
import jax
import jax.numpy as jnp

D = 7168
V = 129280
BISECT_PASSES = 4
PROBES = 4
SEQUENCE_COUNT = 1024


def draw_latent_vectors(key, part):
    key = jax.random.fold_in(key, 11)
    first, second = jax.random.split(key)
    values = jax.random.truncated_normal(first, -6.0, 6.0, (SEQUENCE_COUNT, D), jnp.float32)
    scales = jnp.exp(jax.random.uniform(second, (SEQUENCE_COUNT, 1), jnp.float32, -0.69, 1.38))
    return (values * scales).astype(jnp.bfloat16)


def place_ends(values, key, smallest, high):
    extent = values.shape
    index_at = [jax.random.randint(jax.random.fold_in(key, axis), (), 0, extent[axis]) for axis in range(len(extent))]
    values = values.at[tuple(index_at)].set(smallest)
    longest = extent.index(max(extent))
    index_at[longest] = (index_at[longest] + 1) % extent[longest]
    return values.at[tuple(index_at)].set(high)


def block_scale(own_key, shape, cuts, low, high):
    factor_of = 1.0
    for axis_at, parts in cuts:
        steps = jax.random.uniform(jax.random.fold_in(jax.random.fold_in(own_key, 6), axis_at), (parts,), jnp.float32, low / len(cuts), high / len(cuts))
        factor_of = factor_of * jnp.repeat(jnp.exp(steps), shape[axis_at] // parts).reshape((-1,) + (1,) * (len(shape) - 1 - axis_at))
    return factor_of


def normal_values(key, extent, scale, limit, shards=(), held_as=jnp.bfloat16):
    loudness = block_scale(key, extent, shards, -0.22, 0.18) if shards else 1.0
    array = jax.random.normal(key, extent, jnp.float32) * scale * loudness
    return jnp.minimum(jnp.maximum(array, -limit), limit).astype(held_as)


def setup_inputs(seed: int = 0) -> dict:
    keys = jax.random.split(jax.random.key(seed), 5)
    latent_vectors = draw_latent_vectors(jax.random.fold_in(keys[4], 71), 0)
    unembedding_matrix = normal_values(keys[1], (D, V), 0.0354, 0.19921875, ((1, 128),))
    softmax_divisor = jnp.clip(jnp.exp(math.log(1.5) - 1.0986123 * jax.random.uniform(keys[2], (SEQUENCE_COUNT,), jnp.float32) ** block_scale(keys[2], (SEQUENCE_COUNT,), ((0, 8),), -0.2, 0.2)), 0.5, 1.5)
    top_probability_quota = place_ends(jax.random.randint(keys[3], (SEQUENCE_COUNT,), 50, 100), jax.random.fold_in(keys[3], 1), 50, 99).astype(jnp.int32)
    return {"latent_vectors": latent_vectors, "unembedding_matrix": unembedding_matrix, "softmax_divisor": softmax_divisor, "top_probability_quota": top_probability_quota}


soft_width = 0.25
sharpness = 0.02
initial_level = -16.0
first_spacing = 4.0


def reference(latent_vectors, unembedding_matrix, softmax_divisor, top_probability_quota):
    unnormalized_energies = jnp.dot(latent_vectors, unembedding_matrix, preferred_element_type=jnp.float32) / softmax_divisor[:, None]
    top = jnp.max(unnormalized_energies, axis=1, keepdims=True)
    shifted = unnormalized_energies - top
    expo = jnp.exp(shifted)
    total = jnp.sum(expo, axis=1, keepdims=True)
    prob = expo / total
    level = top_probability_quota.astype(jnp.float32) / 100.0
    lower = jnp.full(level.shape, initial_level, jnp.float32)
    level_spacing = first_spacing
    for round_index in range(BISECT_PASSES):
        passed = jnp.zeros(level.shape, jnp.float32)
        for probe in range(PROBES):
            nucleus_cutoff = lower + level_spacing * (probe + 1)
            mass = jnp.sum(prob * jax.nn.sigmoid((shifted - nucleus_cutoff[:, None]) / soft_width), axis=1)
            passed = passed + jax.nn.sigmoid((mass - level) / sharpness)
        estimate = lower + level_spacing * passed
        level_spacing = level_spacing / 2.0
        lower = estimate - level_spacing
    nucleus_cutoff = lower + 2.0 * level_spacing
    weight = prob * jax.nn.sigmoid((shifted - nucleus_cutoff[:, None]) / soft_width)
    kept = jnp.sum(weight, axis=1, keepdims=True)
    return weight / kept
```

```python
import functools

import jax
import jax.numpy as jnp
from jax import lax
from jax.experimental import pallas as pl
from jax.experimental.pallas import tpu as pltpu
from jax.sharding import PartitionSpec as P

MESH = pl.DeviceIdType.MESH
BISECT_PASSES = 4
PROBES = 4
soft_width = 0.25
sharpness = 0.02
initial_level = -16.0
first_spacing = 4.0

ROWS = 128
HALF = 512
STRIP = 144
NT = (((1,), (1,)), ((), ()))


def wait_bytes(ref, sem):
    pltpu.make_async_copy(ref, ref, sem).wait()


def places():
    dp, vo = lax.axis_index("dp"), lax.axis_index("vocab")
    plane = [(dp, lax.rem(vo + d, 16)) for d in range(1, 16)]
    column = [(lax.rem(dp + 2 * d, 8), vo) for d in range(1, 4)]
    sibling = (dp + 1 - 2 * lax.rem(dp, 2), vo)
    others = [(lax.rem(sibling[0] + 2 * d, 8), vo) for d in range(1, 4)]
    return dp, vo, plane, column, sibling, others


def send(src, dst, send_sem, recv_sem, device):
    copy = pltpu.make_async_remote_copy(
        src_ref=src, dst_ref=dst, send_sem=send_sem, recv_sem=recv_sem, device_id=device, device_id_type=MESH
    )
    copy.start()
    return copy


def fold(fn, init, vocab):
    whole = vocab // STRIP

    def step(t, carry):
        base = pl.multiple_of(t * STRIP, 8)
        for i in range(STRIP // 8):
            carry = fn(carry, pl.ds(base + 8 * i, 8))
        return carry

    return lax.fori_loop(0, whole, step, init)


def exchange(value, join, kind, index, plane, column, bufs, sems):
    out1, in1, out2, in2 = bufs
    send1, recv1, send2, recv2 = sems
    out1[kind, index] = value
    for d, device in enumerate(plane):
        send(out1.at[kind, index], in1.at[kind, index, d], send1.at[kind, index], recv1.at[kind, index], device)
    wait_bytes(in1.at[kind, index], recv1.at[kind, index])
    value = join([value] + [in1[kind, index, d] for d in range(15)])
    out2[kind, index] = value
    for d, device in enumerate(column):
        send(out2.at[kind, index], in2.at[kind, index, d], send2.at[kind, index], recv2.at[kind, index], device)
    wait_bytes(in2.at[kind, index], recv2.at[kind, index])
    return join([value] + [in2[kind, index, d] for d in range(3)])


def total_sum(parts):
    while len(parts) > 1:
        parts = [a + b for a, b in zip(parts[::2], parts[1::2])] + parts[len(parts) & ~1 :]
    return parts[0]


def joined_stats(parts):
    peak = functools.reduce(jnp.maximum, [p[0:1] for p in parts])
    summed = total_sum([p[1:2] * jnp.exp(0.5 * (p[0:1] - peak)) for p in parts])
    return jnp.concatenate([peak, summed], axis=0)


def kernel(
    x_ref, w_ref, div_ref, quota_ref, out_ref, scale_ref,
    xv, wv, logit, half, expo, rowinfo, final,
    so1, si1, so2, si2, mo1, mi1, mo2, mi2, ko1, ki1, ko2, ki2,
    load_sem, row_sem, half_sem, final_sem, s_sems, m_sems, k_sems,
):
    dp, vo, plane, column, sibling, others = places()
    core = lax.rem(dp, 2)
    vocab = w_ref.shape[0]
    depth = w_ref.shape[1]
    load_w = pltpu.make_async_copy(w_ref, wv, load_sem.at[0])
    load_w.start()
    load_x = pltpu.make_async_copy(x_ref, xv, load_sem.at[1])
    load_x.start()

    barrier = pltpu.get_barrier_semaphore()
    greeted = plane + column + [sibling] + others
    for device in greeted:
        pl.semaphore_signal(barrier, inc=1, device_id=device, device_id_type=MESH)
    rowinfo[dp] = jnp.concatenate([2.0 / div_ref[...], quota_ref[...].astype(jnp.float32) / 100.0], axis=0)
    pl.semaphore_wait(barrier, len(greeted))

    for device in column + [sibling] + others:
        send(rowinfo.at[dp], rowinfo.at[dp], row_sem.at[0], row_sem.at[1], device)

    load_w.wait()
    load_x.wait()
    logit[...] = jnp.zeros_like(logit)
    chunk = 1024

    def multiply(k, _):
        cols = pl.ds(pl.multiple_of(k * chunk, chunk), chunk)
        logit[...] += lax.dot_general(wv[:, cols], xv[:, cols], NT, preferred_element_type=jnp.float32)
        return 0

    lax.fori_loop(0, depth // chunk, multiply, 0)
    wait_bytes(rowinfo.at[pl.ds(0, 7)], row_sem.at[1])
    wait_bytes(rowinfo.at[pl.ds(0, 7)], row_sem.at[0])
    copies = []
    for j in range(4):
        block = 2 * j + 1 - core
        cols = pl.ds(pl.multiple_of(block * ROWS, ROWS), ROWS)
        logit[:, cols] = logit[:, cols] * rowinfo[block, 0:1]
        copies.append(
            send(logit.at[:, cols], half.at[1, :, pl.ds(j * ROWS, ROWS)], half_sem.at[0, j], half_sem.at[1, j], sibling)
        )
    level_parts = []
    for j in range(4):
        block = 2 * j + core
        cols = pl.ds(pl.multiple_of(block * ROWS, ROWS), ROWS)
        value = logit[:, cols] * rowinfo[block, 0:1]
        logit[:, cols] = value
        half[0, :, j * ROWS : (j + 1) * ROWS] = value
        level_parts.append(rowinfo[block, 1:2])
    level = jnp.concatenate(level_parts, axis=1)
    for copy in copies:
        copy.wait()

    tail = pl.ds(vocab // 8 * 8, vocab % 8)

    peak = jnp.full((8, HALF), -3e38, jnp.float32)
    for v in range(2):
        peak = fold(lambda c, r: jnp.maximum(c, half[v, r, :]), peak, vocab)
    peak = jnp.max(peak, axis=0, keepdims=True)
    for v in range(2):
        peak = jnp.maximum(peak, jnp.max(half[v, tail, :], axis=0, keepdims=True))
    own_sum = jnp.zeros((8, HALF), jnp.float32)
    wide = jnp.broadcast_to(peak, (8, HALF))
    tail_sum = jnp.zeros((1, HALF), jnp.float32)
    for v in range(2):

        def add_exp(carry, r):
            e = jnp.exp(0.5 * (half[v, r, :] - wide))
            expo[v, r, :] = e
            return carry + e

        own_sum = fold(add_exp, own_sum, vocab)
        e = jnp.exp(0.5 * (half[v, tail, :] - peak))
        expo[v, tail, :] = e
        tail_sum = tail_sum + jnp.sum(e, axis=0, keepdims=True)
    own_sum = jnp.sum(own_sum, axis=0, keepdims=True) + tail_sum
    stats = exchange(
        jnp.concatenate([peak, own_sum], axis=0), joined_stats, 0, 0, plane, column, (so1, si1, so2, si2), s_sems
    )
    top, total = stats[0:1], stats[1:2]
    share = 0.5 * jnp.exp(0.5 * (peak - top)) / total

    def masses(cuts):
        n = len(cuts)
        wides = [jnp.broadcast_to(c, (8, HALF)) for c in cuts]
        sums = tuple(jnp.zeros((8, HALF), jnp.float32) for _ in cuts)
        rest = [jnp.zeros((1, HALF), jnp.float32) for _ in cuts]
        for v in range(2):

            def add(carry, r):
                l, e = half[v, r, :], expo[v, r, :]
                return tuple(carry[k] + e * jnp.tanh(l - wides[k]) for k in range(n))

            sums = fold(add, sums, vocab)
            l, e = half[v, tail, :], expo[v, tail, :]
            rest = [rest[k] + jnp.sum(e * jnp.tanh(l - cuts[k]), axis=0, keepdims=True) for k in range(n)]
        return [share * (own_sum + jnp.sum(sums[k], axis=0, keepdims=True) + rest[k]) for k in range(n)]

    def bisect(r, carry):
        lower, spacing = carry
        parts = masses([top + 2.0 * (lower + spacing * (k + 1)) for k in range(PROBES)])
        mass = exchange(
            jnp.concatenate(parts, axis=0), total_sum, 0, r, plane, column, (mo1, mi1, mo2, mi2), m_sems
        )
        passed = jnp.sum(jax.nn.sigmoid((mass - level) / sharpness), axis=0, keepdims=True)
        estimate = lower + spacing * passed
        spacing = spacing / 2.0
        return estimate - spacing, spacing

    lower, spacing = lax.fori_loop(
        0, BISECT_PASSES, bisect, (jnp.full((1, HALF), initial_level, jnp.float32), jnp.float32(first_spacing))
    )
    cut = top + 2.0 * (lower + 2.0 * spacing)
    final[core, 0:1, :] = top
    final[core, 1:2, :] = cut
    kept = exchange(masses([cut])[0], total_sum, 0, 0, plane, column, (ko1, ki1, ko2, ki2), k_sems)
    final[core, 2:3, :] = 1.0 / (total * kept)
    swap = send(final.at[core], final.at[core], final_sem.at[0], final_sem.at[1], sibling)
    swap.wait()
    for block in range(8):
        h, j = block % 2, block // 2
        lanes = slice(j * ROWS, (j + 1) * ROWS)
        cols = slice(block * ROWS, (block + 1) * ROWS)
        top_b, cut_b, scale_b = (final[h, i : i + 1, lanes] for i in range(3))
        scale_ref[:, cols] = scale_b
        value = logit[:, cols]
        out_ref[:, cols] = jnp.exp(0.5 * (value - top_b)) * (0.5 + 0.5 * jnp.tanh(value - cut_b))

    for ins, sems, count in (((si1, si2), s_sems, 1), ((mi1, mi2), m_sems, BISECT_PASSES), ((ki1, ki2), k_sems, 1)):
        for index in range(count):
            wait_bytes(ins[0].at[0, index], sems[0].at[0, index])
            wait_bytes(ins[1].at[0, index], sems[2].at[0, index])


def slots(count, height):
    f32 = jnp.float32
    return [
        pltpu.VMEM((1, count, height, HALF), f32),
        pltpu.VMEM((1, count, 15, height, HALF), f32),
        pltpu.VMEM((1, count, height, HALF), f32),
        pltpu.VMEM((1, count, 3, height, HALF), f32),
    ]


def on_device(latent_vectors, unembedding_matrix, softmax_divisor, top_probability_quota):
    x = lax.all_gather(latent_vectors, "dp", axis=0, tiled=True)
    weights = unembedding_matrix.T
    vocab, depth = weights.shape
    batch = x.shape[0]
    f32 = jnp.float32
    dma = pltpu.SemaphoreType.DMA
    vmem = pl.BlockSpec(memory_space=pltpu.VMEM)
    hbm = pl.BlockSpec(memory_space=pl.ANY)
    out, scale = pl.pallas_call(
        kernel,
        out_shape=[jax.ShapeDtypeStruct((vocab, batch), f32), jax.ShapeDtypeStruct((1, batch), f32)],
        in_specs=[hbm, hbm, vmem, vmem],
        out_specs=[vmem, vmem],
        scratch_shapes=[
            pltpu.VMEM((batch, depth), jnp.bfloat16),
            pltpu.VMEM((vocab, depth), jnp.bfloat16),
            pltpu.VMEM((vocab, batch), f32),
            pltpu.VMEM((2, vocab, HALF), f32),
            pltpu.VMEM((2, vocab, HALF), f32),
            pltpu.VMEM((8, 2, ROWS), f32),
            pltpu.VMEM((2, 4, HALF), f32),
            *slots(1, 2),
            *slots(BISECT_PASSES, 4),
            *slots(1, 1),
            dma((2,)),
            dma((2,)),
            dma((2, 4)),
            dma((2,)),
            [dma((1, 1))] * 4,
            [dma((1, BISECT_PASSES))] * 4,
            [dma((1, 1))] * 4,
        ],
        compiler_params=pltpu.CompilerParams(
            collective_id=0, has_side_effects=True, vmem_limit_bytes=58 * 1024 * 1024
        ),
        cost_estimate=pl.CostEstimate(
            flops=2 * vocab * depth * batch, bytes_accessed=2 * depth * (vocab + batch), transcendentals=20 * vocab * batch
        ),
    )(x, weights, softmax_divisor[None, :], top_probability_quota[None, :])
    return (out * scale).T


def solution(mesh):
    placed = (P("dp", None), P(None, ("dp", "vocab")), P("dp"), P("dp"))
    return jax.shard_map(
        on_device, mesh=mesh, in_specs=placed, out_specs=P(None, ("dp", "vocab")), check_vma=False
    )
```

```python
import functools

import jax
import jax.numpy as jnp
from jax import lax
from jax.experimental import pallas as pl
from jax.experimental.pallas import tpu as pltpu
from jax.sharding import PartitionSpec as P

MESH = pl.DeviceIdType.MESH
BISECT_PASSES = 4
PROBES = 4
soft_width = 0.25
sharpness = 0.02
initial_level = -16.0
first_spacing = 4.0

ROWS = 128
HALF = 512
STRIP = 144
CHUNKS = 7
UNITS = 4 * CHUNKS
LAG_SHARE = 4
LAG_MULTIPLY = 6
NT = (((1,), (1,)), ((), ()))


def wait_bytes(ref, sem):
    pltpu.make_async_copy(ref, ref, sem).wait()


def places():
    dp, vo = lax.axis_index("dp"), lax.axis_index("vocab")
    plane = [(dp, lax.rem(vo + d, 16)) for d in range(1, 16)]
    column = [(lax.rem(dp + 2 * d, 8), vo) for d in range(1, 4)]
    sibling = (dp + 1 - 2 * lax.rem(dp, 2), vo)
    others = [(lax.rem(sibling[0] + 2 * d, 8), vo) for d in range(1, 4)]
    return dp, vo, plane, column, sibling, others


def send(src, dst, send_sem, recv_sem, device):
    copy = pltpu.make_async_remote_copy(
        src_ref=src, dst_ref=dst, send_sem=send_sem, recv_sem=recv_sem, device_id=device, device_id_type=MESH
    )
    copy.start()
    return copy


def fold(fn, init, vocab):
    whole = vocab // STRIP

    def step(t, carry):
        base = pl.multiple_of(t * STRIP, 8)
        for i in range(STRIP // 8):
            carry = fn(carry, pl.ds(base + 8 * i, 8))
        return carry

    return lax.fori_loop(0, whole, step, init)


def exchange(value, join, kind, index, plane, column, bufs, sems):
    out1, in1, out2, in2 = bufs
    send1, recv1, send2, recv2 = sems
    out1[kind, index] = value
    for d, device in enumerate(plane):
        send(out1.at[kind, index], in1.at[kind, index, d], send1.at[kind, index], recv1.at[kind, index], device)
    wait_bytes(in1.at[kind, index], recv1.at[kind, index])
    value = join([value] + [in1[kind, index, d] for d in range(15)])
    out2[kind, index] = value
    for d, device in enumerate(column):
        send(out2.at[kind, index], in2.at[kind, index, d], send2.at[kind, index], recv2.at[kind, index], device)
    wait_bytes(in2.at[kind, index], recv2.at[kind, index])
    return join([value] + [in2[kind, index, d] for d in range(3)])


def total_sum(parts):
    while len(parts) > 1:
        parts = [a + b for a, b in zip(parts[::2], parts[1::2])] + parts[len(parts) & ~1 :]
    return parts[0]


def joined_stats(parts):
    peak = functools.reduce(jnp.maximum, [p[0:1] for p in parts])
    summed = total_sum([p[1:2] * jnp.exp(0.5 * (p[0:1] - peak)) for p in parts])
    return jnp.concatenate([peak, summed], axis=0)


def kernel(
    x_ref, w_ref, div_ref, quota_ref, out_ref, scale_ref,
    xv, wv, logit, half, expo, rowinfo, final,
    so1, si1, so2, si2, mo1, mi1, mo2, mi2, ko1, ki1, ko2, ki2,
    load_sem, row_sem, y_sem, p_sem, c_sem, half_sem, final_sem, s_sems, m_sems, k_sems,
):
    dp, vo, plane, column, sibling, others = places()
    core = lax.rem(dp, 2)
    vocab = w_ref.shape[0]
    depth = w_ref.shape[1]
    chunk = depth // CHUNKS
    load_x = pltpu.make_async_copy(x_ref, xv.at[pl.ds(pl.multiple_of(dp * ROWS, ROWS), ROWS)], load_sem.at[CHUNKS])
    load_x.start()
    load_w = []
    for k in range(CHUNKS):
        cols = pl.ds(k * chunk, chunk)
        load_w.append(pltpu.make_async_copy(w_ref.at[:, cols], wv.at[:, cols], load_sem.at[k]))
        load_w[k].start()

    barrier = pltpu.get_barrier_semaphore()
    greeted = plane + column + [sibling] + others
    for device in greeted:
        pl.semaphore_signal(barrier, inc=1, device_id=device, device_id_type=MESH)
    rowinfo[dp] = jnp.concatenate([2.0 / div_ref[...], quota_ref[...].astype(jnp.float32) / 100.0], axis=0)
    pl.semaphore_wait(barrier, len(greeted))

    for device in column + [sibling] + others:
        send(rowinfo.at[dp], rowinfo.at[dp], row_sem.at[0], row_sem.at[1], device)

    x_at, z_at = lax.div(vo, 4), lax.rem(vo, 4)
    y_at = lax.div(dp, 2)
    line_z = [(dp, x_at * 4 + lax.rem(z_at + e, 4)) for e in range(1, 4)]
    line_x = [(dp, lax.rem(x_at + e, 4) * 4 + z_at) for e in range(1, 4)]
    first_row = pl.multiple_of(dp * ROWS, ROWS)

    def unit(m):
        i = m - CHUNKS
        near = i < 2 * CHUNKS
        offset = jnp.where(i < 0, 0, jnp.where(near, 1 + 2 * lax.rem(i, 2), 2))
        k = jnp.where(i < 0, m, jnp.where(near, lax.div(i, 2), i - 2 * CHUNKS))
        return offset, pl.ds(pl.multiple_of(k * chunk, chunk), chunk), k

    def pieces(block):
        base = block * ROWS
        return (
            pl.ds(pl.multiple_of(base + 16 * z_at, 16), 16),
            pl.ds(pl.multiple_of(base + 64 + 16 * x_at, 16), 16),
        )

    def spread(m, _):
        offset, cols, _ = unit(m)
        target = (lax.rem(2 * (y_at + 4 - offset) + core, 8), vo)
        for local, there in zip(pieces(0), pieces(dp)):
            send(x_ref.at[local, cols], xv.at[there, cols], y_sem.at[0, m], y_sem.at[1, m], target)
        return 0

    def share_own(m, _):
        _, cols, _ = unit(m)
        send(x_ref.at[:, cols], xv.at[pl.ds(first_row, ROWS), cols], c_sem.at[0, m], c_sem.at[1, m], sibling)
        return 0

    def source_block(offset):
        return lax.rem(2 * (y_at + offset) + core, 8)

    def pass_on(m):
        offset, cols, _ = unit(m)
        wait_bytes(xv.at[pl.ds(0, 32), cols], y_sem.at[1, m])
        for rows, line in zip(pieces(source_block(offset)), (line_z, line_x)):
            for device in line:
                send(xv.at[rows, cols], xv.at[rows, cols], p_sem.at[0, m], p_sem.at[1, m], device)

    def share(m):
        offset, cols, _ = unit(m)
        wait_bytes(xv.at[pl.ds(0, 96), cols], p_sem.at[1, m])
        rows = pl.ds(pl.multiple_of(source_block(offset) * ROWS, ROWS), ROWS)
        send(xv.at[rows, cols], xv.at[rows, cols], c_sem.at[0, m], c_sem.at[1, m], sibling)

    def multiply(m):
        offset, cols, k = unit(m)
        plane_at = lax.rem(y_at + offset, 4)
        rows = pl.ds(pl.multiple_of(plane_at * 2 * ROWS, 2 * ROWS), 2 * ROWS)
        wait_bytes(xv.at[pl.ds(0, ROWS), cols], c_sem.at[1, m])
        logit[:, rows] += lax.dot_general(wv[:, cols], xv[rows, cols], NT, preferred_element_type=jnp.float32)

        @pl.when(k == CHUNKS - 1)
        def _():
            block = 2 * plane_at + 1 - core
            cols = pl.ds(pl.multiple_of(block * ROWS, ROWS), ROWS)
            there = pl.ds(pl.multiple_of(plane_at * ROWS, ROWS), ROWS)
            logit[:, cols] = logit[:, cols] * rowinfo[block, 0:1]
            send(logit.at[:, cols], half.at[1, :, there], half_sem.at[0, plane_at], half_sem.at[1, plane_at], sibling)
            block = 2 * plane_at + core
            cols = pl.ds(pl.multiple_of(block * ROWS, ROWS), ROWS)
            value = logit[:, cols] * rowinfo[block, 0:1]
            logit[:, cols] = value
            half[0, :, there] = value

    lax.fori_loop(0, CHUNKS, share_own, 0)
    lax.fori_loop(CHUNKS, UNITS, spread, 0)
    logit[...] = jnp.zeros_like(logit)
    load_x.wait()
    for m in range(CHUNKS):
        load_w[m].wait()
        if m < CHUNKS - LAG_MULTIPLY:
            multiply(m)
    wait_bytes(rowinfo.at[pl.ds(0, 7)], row_sem.at[1])
    wait_bytes(rowinfo.at[pl.ds(0, 7)], row_sem.at[0])

    def step(t, _):
        @pl.when(t < UNITS)
        def _():
            pass_on(t)

        @pl.when((t >= CHUNKS + LAG_SHARE) & (t < UNITS + LAG_SHARE))
        def _():
            share(t - LAG_SHARE)

        multiply(t - LAG_MULTIPLY)
        return 0

    lax.fori_loop(CHUNKS, UNITS + LAG_MULTIPLY, step, 0)
    level = jnp.concatenate([rowinfo[2 * j + core, 1:2] for j in range(4)], axis=1)
    for j in range(4):
        wait_bytes(half.at[1, :, pl.ds(0, ROWS)], half_sem.at[1, j])

    tail = pl.ds(vocab // 8 * 8, vocab % 8)

    peak = jnp.full((8, HALF), -3e38, jnp.float32)
    for v in range(2):
        peak = fold(lambda c, r: jnp.maximum(c, half[v, r, :]), peak, vocab)
    peak = jnp.max(peak, axis=0, keepdims=True)
    for v in range(2):
        peak = jnp.maximum(peak, jnp.max(half[v, tail, :], axis=0, keepdims=True))
    own_sum = jnp.zeros((8, HALF), jnp.float32)
    wide = jnp.broadcast_to(peak, (8, HALF))
    tail_sum = jnp.zeros((1, HALF), jnp.float32)
    for v in range(2):

        def add_exp(carry, r):
            e = jnp.exp(0.5 * (half[v, r, :] - wide))
            expo[v, r, :] = e
            return carry + e

        own_sum = fold(add_exp, own_sum, vocab)
        e = jnp.exp(0.5 * (half[v, tail, :] - peak))
        expo[v, tail, :] = e
        tail_sum = tail_sum + jnp.sum(e, axis=0, keepdims=True)
    own_sum = jnp.sum(own_sum, axis=0, keepdims=True) + tail_sum
    stats = exchange(
        jnp.concatenate([peak, own_sum], axis=0), joined_stats, 0, 0, plane, column, (so1, si1, so2, si2), s_sems
    )
    top, total = stats[0:1], stats[1:2]
    share = 0.5 * jnp.exp(0.5 * (peak - top)) / total

    def masses(cuts):
        n = len(cuts)
        wides = [jnp.broadcast_to(c, (8, HALF)) for c in cuts]
        sums = tuple(jnp.zeros((8, HALF), jnp.float32) for _ in cuts)
        rest = [jnp.zeros((1, HALF), jnp.float32) for _ in cuts]
        for v in range(2):

            def add(carry, r):
                l, e = half[v, r, :], expo[v, r, :]
                return tuple(carry[k] + e * jnp.tanh(l - wides[k]) for k in range(n))

            sums = fold(add, sums, vocab)
            l, e = half[v, tail, :], expo[v, tail, :]
            rest = [rest[k] + jnp.sum(e * jnp.tanh(l - cuts[k]), axis=0, keepdims=True) for k in range(n)]
        return [share * (own_sum + jnp.sum(sums[k], axis=0, keepdims=True) + rest[k]) for k in range(n)]

    def bisect(r, carry):
        lower, spacing = carry
        parts = masses([top + 2.0 * (lower + spacing * (k + 1)) for k in range(PROBES)])
        mass = exchange(
            jnp.concatenate(parts, axis=0), total_sum, 0, r, plane, column, (mo1, mi1, mo2, mi2), m_sems
        )
        passed = jnp.sum(jax.nn.sigmoid((mass - level) / sharpness), axis=0, keepdims=True)
        estimate = lower + spacing * passed
        spacing = spacing / 2.0
        return estimate - spacing, spacing

    lower, spacing = lax.fori_loop(
        0, BISECT_PASSES, bisect, (jnp.full((1, HALF), initial_level, jnp.float32), jnp.float32(first_spacing))
    )
    cut = top + 2.0 * (lower + 2.0 * spacing)
    final[core, 0:1, :] = top
    final[core, 1:2, :] = cut
    kept = exchange(masses([cut])[0], total_sum, 0, 0, plane, column, (ko1, ki1, ko2, ki2), k_sems)
    final[core, 2:3, :] = 1.0 / (total * kept)
    swap = send(final.at[core], final.at[core], final_sem.at[0], final_sem.at[1], sibling)
    swap.wait()
    for block in range(8):
        h, j = block % 2, block // 2
        lanes = slice(j * ROWS, (j + 1) * ROWS)
        cols = slice(block * ROWS, (block + 1) * ROWS)
        top_b, cut_b, scale_b = (final[h, i : i + 1, lanes] for i in range(3))
        scale_ref[:, cols] = scale_b
        value = logit[:, cols]
        out_ref[:, cols] = jnp.exp(0.5 * (value - top_b)) * (0.5 + 0.5 * jnp.tanh(value - cut_b))

    def left(m, _):
        cols = pl.ds(0, chunk)
        wait_bytes(xv.at[pl.ds(0, ROWS), cols], c_sem.at[0, m])

        @pl.when(m >= CHUNKS)
        def _():
            wait_bytes(xv.at[pl.ds(0, 32), cols], y_sem.at[0, m])
            wait_bytes(xv.at[pl.ds(0, 96), cols], p_sem.at[0, m])

        return 0

    lax.fori_loop(0, UNITS, left, 0)
    for j in range(4):
        wait_bytes(half.at[1, :, pl.ds(0, ROWS)], half_sem.at[0, j])
    for ins, sems, count in (((si1, si2), s_sems, 1), ((mi1, mi2), m_sems, BISECT_PASSES), ((ki1, ki2), k_sems, 1)):
        for index in range(count):
            wait_bytes(ins[0].at[0, index], sems[0].at[0, index])
            wait_bytes(ins[1].at[0, index], sems[2].at[0, index])


def slots(count, height):
    f32 = jnp.float32
    return [
        pltpu.VMEM((1, count, height, HALF), f32),
        pltpu.VMEM((1, count, 15, height, HALF), f32),
        pltpu.VMEM((1, count, height, HALF), f32),
        pltpu.VMEM((1, count, 3, height, HALF), f32),
    ]


def on_device(latent_vectors, unembedding_matrix, softmax_divisor, top_probability_quota):
    weights = unembedding_matrix.T
    vocab, depth = weights.shape
    batch = 8 * ROWS
    f32 = jnp.float32
    dma = pltpu.SemaphoreType.DMA
    vmem = pl.BlockSpec(memory_space=pltpu.VMEM)
    hbm = pl.BlockSpec(memory_space=pl.ANY)
    out, scale = pl.pallas_call(
        kernel,
        out_shape=[jax.ShapeDtypeStruct((vocab, batch), f32), jax.ShapeDtypeStruct((1, batch), f32)],
        in_specs=[hbm, hbm, vmem, vmem],
        out_specs=[vmem, vmem],
        scratch_shapes=[
            pltpu.VMEM((batch, depth), jnp.bfloat16),
            pltpu.VMEM((vocab, depth), jnp.bfloat16),
            pltpu.VMEM((vocab, batch), f32),
            pltpu.VMEM((2, vocab, HALF), f32),
            pltpu.VMEM((2, vocab, HALF), f32),
            pltpu.VMEM((8, 2, ROWS), f32),
            pltpu.VMEM((2, 4, HALF), f32),
            *slots(1, 2),
            *slots(BISECT_PASSES, 4),
            *slots(1, 1),
            dma((CHUNKS + 1,)),
            dma((2,)),
            dma((2, UNITS)),
            dma((2, UNITS)),
            dma((2, UNITS)),
            dma((2, 4)),
            dma((2,)),
            [dma((1, 1))] * 4,
            [dma((1, BISECT_PASSES))] * 4,
            [dma((1, 1))] * 4,
        ],
        compiler_params=pltpu.CompilerParams(
            collective_id=0, has_side_effects=True, vmem_limit_bytes=58 * 1024 * 1024
        ),
        cost_estimate=pl.CostEstimate(
            flops=2 * vocab * depth * batch, bytes_accessed=2 * depth * (vocab + batch), transcendentals=20 * vocab * batch
        ),
    )(latent_vectors, weights, softmax_divisor[None, :], top_probability_quota[None, :])
    return (out * scale).T


def solution(mesh):
    placed = (P("dp", None), P(None, ("dp", "vocab")), P("dp"), P("dp"))
    return jax.shard_map(
        on_device, mesh=mesh, in_specs=placed, out_specs=P(None, ("dp", "vocab")), check_vma=False
    )
```

```python
import functools

import jax
import jax.numpy as jnp
from jax import lax
from jax.experimental import pallas as pl
from jax.experimental.pallas import tpu as pltpu
from jax.sharding import PartitionSpec as P

MESH = pl.DeviceIdType.MESH
BISECT_PASSES = 4
PROBES = 4
soft_width = 0.25
sharpness = 0.02
initial_level = -16.0
first_spacing = 4.0

ROWS = 128
HALF = 512
GROUP = 256
GROUPS = 2
STRIP = 336
CHUNKS = 7
UNITS = 4 * CHUNKS
LAG_FORWARD = 3
LAG_SHARE = 6
LAG_MULTIPLY = 8
EARLY = 4
NT = (((1,), (1,)), ((), ()))


def wait_bytes(ref, sem):
    pltpu.make_async_copy(ref, ref, sem).wait()


def places():
    dp, vo = lax.axis_index("dp"), lax.axis_index("vocab")
    plane = [(dp, lax.rem(vo + d, 16)) for d in range(1, 16)]
    column = [(lax.rem(dp + 2 * d, 8), vo) for d in range(1, 4)]
    sibling = (dp + 1 - 2 * lax.rem(dp, 2), vo)
    others = [(lax.rem(sibling[0] + 2 * d, 8), vo) for d in range(1, 4)]
    return dp, vo, plane, column, sibling, others


def send(src, dst, send_sem, recv_sem, device):
    copy = pltpu.make_async_remote_copy(
        src_ref=src, dst_ref=dst, send_sem=send_sem, recv_sem=recv_sem, device_id=device, device_id_type=MESH
    )
    copy.start()
    return copy


def fold(fn, init, vocab):
    def step(t, carry):
        base = pl.multiple_of(t * STRIP, 8)
        for i in range(STRIP // 8):
            carry = fn(carry, pl.ds(base + 8 * i, 8))
        return carry

    return lax.fori_loop(0, vocab // STRIP, step, init)


def exchange(value, join, trip, plane, column, bufs, sems):
    out1, in1, out2, in2 = bufs
    out1[trip] = value
    for d, device in enumerate(plane):
        send(out1.at[trip], in1.at[trip, d], sems.at[0, trip], sems.at[1, trip], device)
    yield
    wait_bytes(in1.at[trip], sems.at[1, trip])
    value = join([value] + [in1[trip, d] for d in range(15)])
    out2[trip] = value
    for d, device in enumerate(column):
        send(out2.at[trip], in2.at[trip, d], sems.at[2, trip], sems.at[3, trip], device)
    yield
    wait_bytes(in2.at[trip], sems.at[3, trip])
    return join([value] + [in2[trip, d] for d in range(3)])


def total_sum(parts):
    while len(parts) > 1:
        parts = [a + b for a, b in zip(parts[::2], parts[1::2])] + parts[len(parts) & ~1 :]
    return parts[0]


def joined_stats(parts):
    peak = functools.reduce(jnp.maximum, [p[0:1] for p in parts])
    summed = total_sum([p[1:2] * jnp.exp(0.5 * (p[0:1] - peak)) for p in parts])
    return jnp.concatenate([peak, summed], axis=0)


def kernel(
    x_ref, w_ref, div_ref, quota_ref, out_ref, scale_ref,
    xv, wv, logit, half, expo, rowinfo, final, scale,
    stat_bufs, mass_bufs, kept_bufs,
    load_sem, row_sem, y_sem, p_sem, f_sem, c_sem, half_sem, final_sem, stat_sem, mass_sem, kept_sem,
):
    dp, vo, plane, column, sibling, others = places()
    core = lax.rem(dp, 2)
    vocab = w_ref.shape[0]
    depth = w_ref.shape[1]
    chunk = depth // CHUNKS
    load_x = pltpu.make_async_copy(x_ref, xv.at[pl.ds(pl.multiple_of(dp * ROWS, ROWS), ROWS)], load_sem.at[CHUNKS])
    load_x.start()
    load_w = []
    for k in range(CHUNKS):
        cols = pl.ds(k * chunk, chunk)
        load_w.append(pltpu.make_async_copy(w_ref.at[:, cols], wv.at[:, cols], load_sem.at[k]))
        load_w[k].start()

    barrier = pltpu.get_barrier_semaphore()
    greeted = plane + column + [sibling] + others
    for device in greeted:
        pl.semaphore_signal(barrier, inc=1, device_id=device, device_id_type=MESH)
    rowinfo[dp] = jnp.concatenate([2.0 / div_ref[...], quota_ref[...].astype(jnp.float32) / 100.0], axis=0)
    pl.semaphore_wait(barrier, len(greeted))

    for device in column + [sibling] + others:
        send(rowinfo.at[dp], rowinfo.at[dp], row_sem.at[0], row_sem.at[1], device)

    x_at, z_at = lax.div(vo, 4), lax.rem(vo, 4)
    y_at = lax.div(dp, 2)
    line_z = [(dp, x_at * 4 + lax.rem(z_at + e, 4)) for e in range(1, 4)]
    line_x = [(dp, lax.rem(x_at + e, 4) * 4 + z_at) for e in range(1, 4)]
    first_row = pl.multiple_of(dp * ROWS, ROWS)

    def unit(m):
        i = m - CHUNKS
        near = i < 2 * CHUNKS
        offset = jnp.where(i < 0, 0, jnp.where(near, 1 + 2 * lax.rem(i, 2), 2))
        k = jnp.where(i < 0, m, jnp.where(near, lax.div(i, 2), i - 2 * CHUNKS))
        return offset, pl.ds(pl.multiple_of(k * chunk, chunk), chunk), k

    def pieces(block):
        base = block * ROWS
        return (
            pl.ds(pl.multiple_of(base + 16 * z_at, 16), 16),
            pl.ds(pl.multiple_of(base + 64 + 16 * x_at, 16), 16),
        )

    def spread(m, _):
        offset, cols, _ = unit(m)
        target = (lax.rem(2 * (y_at + 4 - offset) + core, 8), vo)
        for local, there in zip(pieces(0), pieces(dp)):
            send(x_ref.at[local, cols], xv.at[there, cols], y_sem.at[0, m], y_sem.at[1, m], target)
        return 0

    def share_own(m, _):
        _, cols, _ = unit(m)
        send(x_ref.at[:, cols], xv.at[pl.ds(first_row, ROWS), cols], c_sem.at[0, m], c_sem.at[1, m], sibling)
        return 0

    def source_block(offset):
        return lax.rem(2 * (y_at + offset) + core, 8)

    def pass_on(m):
        offset, cols, _ = unit(m)
        wait_bytes(xv.at[pl.ds(0, 32), cols], y_sem.at[1, m])
        for rows, line in zip(pieces(source_block(offset)), (line_z, line_x)):
            for device in (line[0], line[2]):
                send(xv.at[rows, cols], xv.at[rows, cols], p_sem.at[0, m], p_sem.at[1, m], device)

    def forward(m):
        offset, cols, k = unit(m)
        wait_bytes(xv.at[pl.ds(0, 64), cols], p_sem.at[1, m])
        base = source_block(offset) * ROWS
        for at, shift, line in ((z_at, 0, line_z), (x_at, 64, line_x)):
            for part, (step, device) in enumerate(((3, line[0]), (1, line[2]))):
                rows = pl.ds(pl.multiple_of(base + shift + 16 * lax.rem(at + step, 4), 16), 16)
                cols = pl.ds(pl.multiple_of(k * chunk + part * (chunk // 2), chunk // 2), chunk // 2)
                send(xv.at[rows, cols], xv.at[rows, cols], f_sem.at[0, m], f_sem.at[1, m], device)

    def share(m):
        offset, cols, _ = unit(m)
        wait_bytes(xv.at[pl.ds(0, 32), cols], f_sem.at[1, m])
        rows = pl.ds(pl.multiple_of(source_block(offset) * ROWS, ROWS), ROWS)
        send(xv.at[rows, cols], xv.at[rows, cols], c_sem.at[0, m], c_sem.at[1, m], sibling)

    def multiply(m):
        offset, cols, k = unit(m)
        plane_at = lax.rem(y_at + offset, 4)
        rows = pl.ds(pl.multiple_of(plane_at * 2 * ROWS, 2 * ROWS), 2 * ROWS)
        wait_bytes(xv.at[pl.ds(0, ROWS), cols], c_sem.at[1, m])
        logit[:, rows] += lax.dot_general(wv[:, cols], xv[rows, cols], NT, preferred_element_type=jnp.float32)

        @pl.when(k == CHUNKS - 1)
        def _():
            block = 2 * plane_at + 1 - core
            cols = pl.ds(pl.multiple_of(block * ROWS, ROWS), ROWS)
            there = pl.ds(pl.multiple_of(plane_at * ROWS, ROWS), ROWS)
            logit[:, cols] = logit[:, cols] * rowinfo[block, 0:1]
            send(logit.at[:, cols], half.at[1, :, there], half_sem.at[0, plane_at], half_sem.at[1, plane_at], sibling)
            block = 2 * plane_at + core
            cols = pl.ds(pl.multiple_of(block * ROWS, ROWS), ROWS)
            value = logit[:, cols] * rowinfo[block, 0:1]
            logit[:, cols] = value
            half[0, :, there] = value

    lax.fori_loop(0, CHUNKS, share_own, 0)
    lax.fori_loop(CHUNKS, UNITS, spread, 0)
    logit[...] = jnp.zeros_like(logit)
    load_x.wait()
    for m in range(EARLY):
        load_w[m].wait()
        multiply(m)
    wait_bytes(rowinfo.at[pl.ds(0, 7)], row_sem.at[1])
    wait_bytes(rowinfo.at[pl.ds(0, 7)], row_sem.at[0])

    def step(t, _):
        @pl.when(t < UNITS)
        def _():
            pass_on(t)

        @pl.when((t >= CHUNKS + LAG_FORWARD) & (t < UNITS + LAG_FORWARD))
        def _():
            forward(t - LAG_FORWARD)

        @pl.when((t >= CHUNKS + LAG_SHARE) & (t < UNITS + LAG_SHARE))
        def _():
            share(t - LAG_SHARE)

        m = t - LAG_MULTIPLY

        @pl.when((m >= EARLY) & (m < CHUNKS))
        def _():
            wait_bytes(wv.at[:, pl.ds(0, chunk)], load_sem.at[m])

        @pl.when(m >= EARLY)
        def _():
            multiply(m)

        return 0

    lax.fori_loop(CHUNKS, UNITS + LAG_MULTIPLY, step, 0)
    level = jnp.concatenate([rowinfo[2 * j + core, 1:2] for j in range(4)], axis=1)
    for j in range(4):
        wait_bytes(half.at[1, :, pl.ds(0, ROWS)], half_sem.at[1, j])

    tail = pl.ds(vocab // 8 * 8, vocab % 8)

    def follow(g):
        lanes = slice(g * GROUP, (g + 1) * GROUP)

        peak = jnp.full((8, GROUP), -3e38, jnp.float32)
        for v in range(2):
            peak = fold(lambda c, r: jnp.maximum(c, half[v, r, lanes]), peak, vocab)
        peak = jnp.max(peak, axis=0, keepdims=True)
        for v in range(2):
            peak = jnp.maximum(peak, jnp.max(half[v, tail, lanes], axis=0, keepdims=True))
        own_sum = jnp.zeros((8, GROUP), jnp.float32)
        wide = jnp.broadcast_to(peak, (8, GROUP))
        tail_sum = jnp.zeros((1, GROUP), jnp.float32)
        for v in range(2):

            def add_exp(carry, r):
                e = jnp.exp(0.5 * (half[v, r, lanes] - wide))
                expo[v, r, lanes] = e
                return carry + e

            own_sum = fold(add_exp, own_sum, vocab)
            e = jnp.exp(0.5 * (half[v, tail, lanes] - peak))
            expo[v, tail, lanes] = e
            tail_sum = tail_sum + jnp.sum(e, axis=0, keepdims=True)
        own_sum = jnp.sum(own_sum, axis=0, keepdims=True) + tail_sum
        stats = yield from exchange(
            jnp.concatenate([peak, own_sum], axis=0), joined_stats, g, plane, column, stat_bufs, stat_sem
        )
        top, total = stats[0:1], stats[1:2]
        share = 0.5 * jnp.exp(0.5 * (peak - top)) / total

        def masses(cuts):
            n = len(cuts)
            wides = [jnp.broadcast_to(c, (8, GROUP)) for c in cuts]
            sums = tuple(jnp.zeros((8, GROUP), jnp.float32) for _ in cuts)
            rest = [jnp.zeros((1, GROUP), jnp.float32) for _ in cuts]
            for v in range(2):

                def add(carry, r):
                    l, e = half[v, r, lanes], expo[v, r, lanes]
                    return tuple(carry[k] + e * jnp.tanh(l - wides[k]) for k in range(n))

                sums = fold(add, sums, vocab)
                l, e = half[v, tail, lanes], expo[v, tail, lanes]
                rest = [rest[k] + jnp.sum(e * jnp.tanh(l - cuts[k]), axis=0, keepdims=True) for k in range(n)]
            parts = [share * (own_sum + jnp.sum(sums[k], axis=0, keepdims=True) + rest[k]) for k in range(n)]
            return jnp.concatenate(parts, axis=0)

        lower, spacing = jnp.full((1, GROUP), initial_level, jnp.float32), first_spacing
        for r in range(BISECT_PASSES):
            parts = masses([top + 2.0 * (lower + spacing * (k + 1)) for k in range(PROBES)])
            mass = yield from exchange(
                parts, total_sum, r * GROUPS + g, plane, column, mass_bufs, mass_sem
            )
            passed = jnp.sum(jax.nn.sigmoid((mass - level[:, lanes]) / sharpness), axis=0, keepdims=True)
            estimate = lower + spacing * passed
            spacing = spacing / 2.0
            lower = estimate - spacing
        cut = top + 2.0 * (lower + 2.0 * spacing)
        final[core, 0:1, lanes] = top
        final[core, 1:2, lanes] = cut
        here = final.at[core, :, pl.ds(g * GROUP, GROUP)]
        send(here, here, final_sem.at[0, g], final_sem.at[1, g], sibling)
        kept = yield from exchange(masses([cut]), total_sum, g, plane, column, kept_bufs, kept_sem)
        scale[core, 0:1, lanes] = 1.0 / (total * kept)

    def weigh(h, g):
        for j in (2 * g, 2 * g + 1):
            lanes = slice(j * ROWS, (j + 1) * ROWS)
            cols = pl.ds(pl.multiple_of((2 * j + h) * ROWS, ROWS), ROWS)
            top, cut = final[h, 0:1, lanes], final[h, 1:2, lanes]
            value = logit[:, cols]
            out_ref[:, cols] = jnp.exp(0.5 * (value - top)) * (0.5 + 0.5 * jnp.tanh(value - cut))

    rows_of = [follow(g) for g in range(GROUPS)]
    for _ in range(BISECT_PASSES + 1):
        for part in range(2):
            for rows in rows_of:
                next(rows)
    for rows in rows_of:
        next(rows)
    for g in range(GROUPS):
        weigh(core, g)
    for g in range(GROUPS):
        wait_bytes(final.at[core, :, pl.ds(g * GROUP, GROUP)], final_sem.at[1, g])
        weigh(1 - core, g)
    for rows in rows_of:
        next(rows)
    for rows in rows_of:
        next(rows, None)
    swap = send(scale.at[core], scale.at[core], final_sem.at[0, GROUPS], final_sem.at[1, GROUPS], sibling)
    swap.wait()
    for block in range(8):
        lanes = slice(block // 2 * ROWS, (block // 2 + 1) * ROWS)
        scale_ref[:, block * ROWS : (block + 1) * ROWS] = scale[block % 2, :, lanes]

    def left(m, _):
        cols = pl.ds(0, chunk)
        wait_bytes(xv.at[pl.ds(0, ROWS), cols], c_sem.at[0, m])

        @pl.when(m >= CHUNKS)
        def _():
            wait_bytes(xv.at[pl.ds(0, 32), cols], y_sem.at[0, m])
            wait_bytes(xv.at[pl.ds(0, 64), cols], p_sem.at[0, m])
            wait_bytes(xv.at[pl.ds(0, 32), cols], f_sem.at[0, m])

        return 0

    lax.fori_loop(0, UNITS, left, 0)
    for j in range(4):
        wait_bytes(half.at[1, :, pl.ds(0, ROWS)], half_sem.at[0, j])
    for g in range(GROUPS):
        wait_bytes(final.at[core, :, pl.ds(g * GROUP, GROUP)], final_sem.at[0, g])
    for (_, in1, _, in2), sems in ((stat_bufs, stat_sem), (mass_bufs, mass_sem), (kept_bufs, kept_sem)):
        for trip in range(in1.shape[0]):
            wait_bytes(in1.at[trip], sems.at[0, trip])
            wait_bytes(in2.at[trip], sems.at[2, trip])


def slots(count, height):
    f32 = jnp.float32
    return [
        pltpu.VMEM((count, height, GROUP), f32),
        pltpu.VMEM((count, 15, height, GROUP), f32),
        pltpu.VMEM((count, height, GROUP), f32),
        pltpu.VMEM((count, 3, height, GROUP), f32),
    ]


def on_device(latent_vectors, unembedding_matrix, softmax_divisor, top_probability_quota):
    weights = unembedding_matrix.T
    vocab, depth = weights.shape
    batch = 8 * ROWS
    f32 = jnp.float32
    dma = pltpu.SemaphoreType.DMA
    vmem = pl.BlockSpec(memory_space=pltpu.VMEM)
    hbm = pl.BlockSpec(memory_space=pl.ANY)
    out, scale = pl.pallas_call(
        kernel,
        out_shape=[jax.ShapeDtypeStruct((vocab, batch), f32), jax.ShapeDtypeStruct((1, batch), f32)],
        in_specs=[hbm, hbm, vmem, vmem],
        out_specs=[vmem, vmem],
        scratch_shapes=[
            pltpu.VMEM((batch, depth), jnp.bfloat16),
            pltpu.VMEM((vocab, depth), jnp.bfloat16),
            pltpu.VMEM((vocab, batch), f32),
            pltpu.VMEM((2, vocab, HALF), f32),
            pltpu.VMEM((2, vocab, HALF), f32),
            pltpu.VMEM((8, 2, ROWS), f32),
            pltpu.VMEM((2, 2, HALF), f32),
            pltpu.VMEM((2, 1, HALF), f32),
            slots(GROUPS, 2),
            slots(GROUPS * BISECT_PASSES, 4),
            slots(GROUPS, 1),
            dma((CHUNKS + 1,)),
            dma((2,)),
            dma((2, UNITS)),
            dma((2, UNITS)),
            dma((2, UNITS)),
            dma((2, UNITS)),
            dma((2, 4)),
            dma((2, GROUPS + 1)),
            dma((4, GROUPS)),
            dma((4, GROUPS * BISECT_PASSES)),
            dma((4, GROUPS)),
        ],
        compiler_params=pltpu.CompilerParams(
            collective_id=0, has_side_effects=True, vmem_limit_bytes=58 * 1024 * 1024
        ),
        cost_estimate=pl.CostEstimate(
            flops=2 * vocab * depth * batch, bytes_accessed=2 * depth * (vocab + batch), transcendentals=20 * vocab * batch
        ),
    )(latent_vectors, weights, softmax_divisor[None, :], top_probability_quota[None, :])
    return (out * scale).T


def solution(mesh):
    placed = (P("dp", None), P(None, ("dp", "vocab")), P("dp"), P("dp"))
    return jax.shard_map(
        on_device, mesh=mesh, in_specs=placed, out_specs=P(None, ("dp", "vocab")), check_vma=False
    )
```

```python
import functools

import jax
import jax.numpy as jnp
from jax import lax
from jax.experimental import pallas as pl
from jax.experimental.pallas import tpu as pltpu
from jax.sharding import PartitionSpec as P

MESH = pl.DeviceIdType.MESH
BISECT_PASSES = 4
PROBES = 4
soft_width = 0.25
sharpness = 0.02
initial_level = -16.0
first_spacing = 4.0

ROWS = 128
HALF = 512
GROUP = 128
GROUPS = 4
STRIP = 336
CHUNKS = 4
UNITS = 4 * CHUNKS
LAG_FORWARD = 2
LAG_SHARE = 4
LAG_MULTIPLY = 5
EARLY = 1
NT = (((1,), (1,)), ((), ()))


def wait_bytes(ref, sem):
    pltpu.make_async_copy(ref, ref, sem).wait()


def places():
    dp, vo = lax.axis_index("dp"), lax.axis_index("vocab")
    plane = [(dp, lax.rem(vo + d, 16)) for d in range(1, 16)]
    column = [(lax.rem(dp + 2 * d, 8), vo) for d in range(1, 4)]
    sibling = (dp + 1 - 2 * lax.rem(dp, 2), vo)
    x_at, z_at = lax.div(vo, 4), lax.rem(vo, 4)
    line_z = [(dp, x_at * 4 + lax.rem(z_at + e, 4)) for e in range(1, 4)]
    line_x = [(dp, lax.rem(x_at + e, 4) * 4 + z_at) for e in range(1, 4)]
    return dp, x_at, z_at, plane, column, sibling, line_z, line_x


def send(src, dst, send_sem, recv_sem, device):
    copy = pltpu.make_async_remote_copy(
        src_ref=src, dst_ref=dst, send_sem=send_sem, recv_sem=recv_sem, device_id=device, device_id_type=MESH
    )
    copy.start()
    return copy


def fold(fn, init, vocab):
    def step(t, carry):
        base = pl.multiple_of(t * STRIP, 8)
        for i in range(STRIP // 8):
            carry = fn(carry, pl.ds(base + 8 * i, 8))
        return carry

    return lax.fori_loop(0, vocab // STRIP, step, init)


def exchange(value, join, trip, plane, column, bufs, sems):
    out1, in1, out2, in2 = bufs
    out1[trip] = value
    for d, device in enumerate(plane):
        send(out1.at[trip], in1.at[trip, d], sems.at[0, trip], sems.at[1, trip], device)
    yield
    wait_bytes(in1.at[trip], sems.at[1, trip])
    value = join([value] + [in1[trip, d] for d in range(15)])
    out2[trip] = value
    for d, device in enumerate(column):
        send(out2.at[trip], in2.at[trip, d], sems.at[2, trip], sems.at[3, trip], device)
    yield
    wait_bytes(in2.at[trip], sems.at[3, trip])
    return join([value] + [in2[trip, d] for d in range(3)])


def total_sum(parts):
    while len(parts) > 1:
        parts = [a + b for a, b in zip(parts[::2], parts[1::2])] + parts[len(parts) & ~1 :]
    return parts[0]


def joined_stats(parts):
    peak = functools.reduce(jnp.maximum, [p[0:1] for p in parts])
    summed = total_sum([p[1:2] * jnp.exp(0.5 * (p[0:1] - peak)) for p in parts])
    return jnp.concatenate([peak, summed], axis=0)


def kernel(
    x_ref, w_ref, div_ref, quota_ref, out_ref, scale_ref,
    xv, wv, logit, half, expo, rowinfo, final, scale,
    stat_bufs, mass_bufs, kept_bufs,
    plane_sem, load_sem, row_sem, y_sem, p_sem, f_sem, c_sem, half_sem, final_sem, stat_sem, mass_sem, kept_sem,
):
    dp, x_at, z_at, plane, column, sibling, line_z, line_x = places()
    y_at = lax.div(dp, 2)
    core = lax.rem(dp, 2)
    vocab = w_ref.shape[0]
    depth = w_ref.shape[1]
    chunk = depth // CHUNKS
    load_x = pltpu.make_async_copy(x_ref, xv.at[pl.ds(pl.multiple_of(dp * ROWS, ROWS), ROWS)], load_sem.at[CHUNKS])
    load_x.start()
    load_w = []
    for k in range(CHUNKS):
        cols = pl.ds(k * chunk, chunk)
        load_w.append(pltpu.make_async_copy(w_ref.at[:, cols], wv.at[:, cols], load_sem.at[k]))
        load_w[k].start()

    barrier = pltpu.get_barrier_semaphore()
    greeted = line_z + line_x + column + [sibling]
    for device in greeted:
        pl.semaphore_signal(barrier, inc=1, device_id=device, device_id_type=MESH)
    rowinfo[core, y_at] = jnp.concatenate([2.0 / div_ref[...], quota_ref[...].astype(jnp.float32) / 100.0], axis=0)
    pl.semaphore_wait(barrier, len(greeted))

    for device in line_x:
        pl.semaphore_signal(plane_sem, inc=1, device_id=device, device_id_type=MESH)
    for device in column:
        send(rowinfo.at[core, y_at], rowinfo.at[core, y_at], row_sem.at[0], row_sem.at[1], device)

    first_row = pl.multiple_of(dp * ROWS, ROWS)

    def unit(m):
        i = m - CHUNKS
        near = i < 2 * CHUNKS
        offset = jnp.where(i < 0, 0, jnp.where(near, 1 + 2 * lax.rem(i, 2), 2))
        k = jnp.where(i < 0, m, jnp.where(near, lax.div(i, 2), i - 2 * CHUNKS))
        return offset, pl.ds(pl.multiple_of(k * chunk, chunk), chunk), k

    def pieces(block):
        base = block * ROWS
        return (
            pl.ds(pl.multiple_of(base + 16 * z_at, 16), 16),
            pl.ds(pl.multiple_of(base + 64 + 16 * x_at, 16), 16),
        )

    def spread(m, _):
        offset, cols, _ = unit(m)
        target = (lax.rem(2 * (y_at + 4 - offset) + core, 8), column[0][1])
        for local, there in zip(pieces(0), pieces(dp)):
            send(x_ref.at[local, cols], xv.at[there, cols], y_sem.at[0, m], y_sem.at[1, m], target)
        return 0

    def share_own(m, _):
        _, cols, _ = unit(m)
        send(x_ref.at[:, cols], xv.at[pl.ds(first_row, ROWS), cols], c_sem.at[0, m], c_sem.at[1, m], sibling)
        return 0

    def source_block(offset):
        return lax.rem(2 * (y_at + offset) + core, 8)

    def pass_on(m):
        offset, cols, _ = unit(m)
        wait_bytes(xv.at[pl.ds(0, 32), cols], y_sem.at[1, m])
        for rows, line in zip(pieces(source_block(offset)), (line_z, line_x)):
            for device in (line[0], line[2]):
                send(xv.at[rows, cols], xv.at[rows, cols], p_sem.at[0, m], p_sem.at[1, m], device)

    def forward(m):
        offset, cols, k = unit(m)
        wait_bytes(xv.at[pl.ds(0, 64), cols], p_sem.at[1, m])
        base = source_block(offset) * ROWS
        for at, shift, line in ((z_at, 0, line_z), (x_at, 64, line_x)):
            for part, (step, device) in enumerate(((3, line[0]), (1, line[2]))):
                rows = pl.ds(pl.multiple_of(base + shift + 16 * lax.rem(at + step, 4), 16), 16)
                cols = pl.ds(pl.multiple_of(k * chunk + part * (chunk // 2), chunk // 2), chunk // 2)
                send(xv.at[rows, cols], xv.at[rows, cols], f_sem.at[0, m], f_sem.at[1, m], device)

    def share(m):
        offset, cols, _ = unit(m)
        wait_bytes(xv.at[pl.ds(0, 32), cols], f_sem.at[1, m])
        rows = pl.ds(pl.multiple_of(source_block(offset) * ROWS, ROWS), ROWS)
        send(xv.at[rows, cols], xv.at[rows, cols], c_sem.at[0, m], c_sem.at[1, m], sibling)

    def multiply(m):
        offset, cols, k = unit(m)
        plane_at = lax.rem(y_at + offset, 4)
        rows = pl.ds(pl.multiple_of(plane_at * 2 * ROWS, 2 * ROWS), 2 * ROWS)
        wait_bytes(xv.at[pl.ds(0, ROWS), cols], c_sem.at[1, m])
        logit[:, rows] += lax.dot_general(wv[:, cols], xv[rows, cols], NT, preferred_element_type=jnp.float32)

        @pl.when(k == CHUNKS - 1)
        def _():
            block = 2 * plane_at + 1 - core
            cols = pl.ds(pl.multiple_of(block * ROWS, ROWS), ROWS)
            there = pl.ds(pl.multiple_of(plane_at * ROWS, ROWS), ROWS)
            logit[:, cols] = logit[:, cols] * rowinfo[1 - core, plane_at, 0:1]
            send(logit.at[:, cols], half.at[1, :, there], half_sem.at[0, plane_at], half_sem.at[1, plane_at], sibling)
            block = 2 * plane_at + core
            cols = pl.ds(pl.multiple_of(block * ROWS, ROWS), ROWS)
            value = logit[:, cols] * rowinfo[core, plane_at, 0:1]
            logit[:, cols] = value
            half[0, :, there] = value

    lax.fori_loop(0, CHUNKS, share_own, 0)
    lax.fori_loop(CHUNKS, UNITS, spread, 0)
    logit[...] = jnp.zeros_like(logit)
    load_x.wait()
    for m in range(EARLY):
        load_w[m].wait()
        multiply(m)
    wait_bytes(rowinfo.at[0, pl.ds(0, 3)], row_sem.at[1])
    wait_bytes(rowinfo.at[0, pl.ds(0, 3)], row_sem.at[0])
    send(rowinfo.at[core], rowinfo.at[core], row_sem.at[2], row_sem.at[3], sibling)

    def step(t, _):
        @pl.when(t < UNITS)
        def _():
            pass_on(t)

        @pl.when((t >= CHUNKS + LAG_FORWARD) & (t < UNITS + LAG_FORWARD))
        def _():
            forward(t - LAG_FORWARD)

        @pl.when((t >= CHUNKS + LAG_SHARE) & (t < UNITS + LAG_SHARE))
        def _():
            share(t - LAG_SHARE)

        m = t - LAG_MULTIPLY

        @pl.when(m == EARLY)
        def _():
            wait_bytes(rowinfo.at[0], row_sem.at[3])

        @pl.when((m >= EARLY) & (m < CHUNKS))
        def _():
            wait_bytes(wv.at[:, pl.ds(0, chunk)], load_sem.at[m])

        @pl.when(m >= EARLY)
        def _():
            multiply(m)

        return 0

    lax.fori_loop(CHUNKS, UNITS + LAG_MULTIPLY, step, 0)
    pl.semaphore_wait(plane_sem, 3)
    level = jnp.concatenate([rowinfo[core, j, 1:2] for j in range(4)], axis=1)
    for j in range(4):
        wait_bytes(half.at[1, :, pl.ds(0, ROWS)], half_sem.at[1, j])

    tail = pl.ds(vocab // 8 * 8, vocab % 8)

    def follow(g):
        lanes = slice(g * GROUP, (g + 1) * GROUP)

        peak = jnp.full((8, GROUP), -3e38, jnp.float32)
        for v in range(2):
            peak = fold(lambda c, r: jnp.maximum(c, half[v, r, lanes]), peak, vocab)
        peak = jnp.max(peak, axis=0, keepdims=True)
        for v in range(2):
            peak = jnp.maximum(peak, jnp.max(half[v, tail, lanes], axis=0, keepdims=True))
        own_sum = jnp.zeros((8, GROUP), jnp.float32)
        wide = jnp.broadcast_to(peak, (8, GROUP))
        tail_sum = jnp.zeros((1, GROUP), jnp.float32)
        for v in range(2):

            def add_exp(carry, r):
                e = jnp.exp(0.5 * (half[v, r, lanes] - wide))
                expo[v, r, lanes] = e
                return carry + e

            own_sum = fold(add_exp, own_sum, vocab)
            e = jnp.exp(0.5 * (half[v, tail, lanes] - peak))
            expo[v, tail, lanes] = e
            tail_sum = tail_sum + jnp.sum(e, axis=0, keepdims=True)
        own_sum = jnp.sum(own_sum, axis=0, keepdims=True) + tail_sum
        stats = yield from exchange(
            jnp.concatenate([peak, own_sum], axis=0), joined_stats, g, plane, column, stat_bufs, stat_sem
        )
        top, total = stats[0:1], stats[1:2]
        share = 0.5 * jnp.exp(0.5 * (peak - top)) / total

        def masses(cuts):
            n = len(cuts)
            wides = [jnp.broadcast_to(c, (8, GROUP)) for c in cuts]
            sums = tuple(jnp.zeros((8, GROUP), jnp.float32) for _ in cuts)
            rest = [jnp.zeros((1, GROUP), jnp.float32) for _ in cuts]
            for v in range(2):

                def add(carry, r):
                    l, e = half[v, r, lanes], expo[v, r, lanes]
                    return tuple(carry[k] + e * jnp.tanh(l - wides[k]) for k in range(n))

                sums = fold(add, sums, vocab)
                l, e = half[v, tail, lanes], expo[v, tail, lanes]
                rest = [rest[k] + jnp.sum(e * jnp.tanh(l - cuts[k]), axis=0, keepdims=True) for k in range(n)]
            parts = [share * (own_sum + jnp.sum(sums[k], axis=0, keepdims=True) + rest[k]) for k in range(n)]
            return jnp.concatenate(parts, axis=0)

        lower, spacing = jnp.full((1, GROUP), initial_level, jnp.float32), first_spacing
        for r in range(BISECT_PASSES):
            parts = masses([top + 2.0 * (lower + spacing * (k + 1)) for k in range(PROBES)])
            mass = yield from exchange(
                parts, total_sum, r * GROUPS + g, plane, column, mass_bufs, mass_sem
            )
            passed = jnp.sum(jax.nn.sigmoid((mass - level[:, lanes]) / sharpness), axis=0, keepdims=True)
            estimate = lower + spacing * passed
            spacing = spacing / 2.0
            lower = estimate - spacing
        cut = top + 2.0 * (lower + 2.0 * spacing)
        final[core, 0:1, lanes] = top
        final[core, 1:2, lanes] = cut
        here = final.at[core, :, pl.ds(g * GROUP, GROUP)]
        send(here, here, final_sem.at[0, g], final_sem.at[1, g], sibling)
        kept = yield from exchange(masses([cut]), total_sum, g, plane, column, kept_bufs, kept_sem)
        scale[core, 0:1, lanes] = 1.0 / (total * kept)

    def weigh(h, g):
        for j in range(g * GROUP // ROWS, (g + 1) * GROUP // ROWS):
            lanes = slice(j * ROWS, (j + 1) * ROWS)
            cols = pl.ds(pl.multiple_of((2 * j + h) * ROWS, ROWS), ROWS)
            top, cut = final[h, 0:1, lanes], final[h, 1:2, lanes]
            value = logit[:, cols]
            out_ref[:, cols] = jnp.exp(0.5 * (value - top)) * (0.5 + 0.5 * jnp.tanh(value - cut))

    rows_of = [follow(g) for g in range(GROUPS)]
    for _ in range(BISECT_PASSES + 1):
        for part in range(2):
            for rows in rows_of:
                next(rows)
    for rows in rows_of:
        next(rows)
    for g in range(GROUPS):
        weigh(core, g)
    for g in range(GROUPS):
        wait_bytes(final.at[core, :, pl.ds(g * GROUP, GROUP)], final_sem.at[1, g])
        weigh(1 - core, g)
    for rows in rows_of:
        next(rows)
    for rows in rows_of:
        next(rows, None)
    swap = send(scale.at[core], scale.at[core], final_sem.at[0, GROUPS], final_sem.at[1, GROUPS], sibling)
    swap.wait()
    for block in range(8):
        lanes = slice(block // 2 * ROWS, (block // 2 + 1) * ROWS)
        scale_ref[:, block * ROWS : (block + 1) * ROWS] = scale[block % 2, :, lanes]

    def left(m, _):
        cols = pl.ds(0, chunk)
        wait_bytes(xv.at[pl.ds(0, ROWS), cols], c_sem.at[0, m])

        @pl.when(m >= CHUNKS)
        def _():
            wait_bytes(xv.at[pl.ds(0, 32), cols], y_sem.at[0, m])
            wait_bytes(xv.at[pl.ds(0, 64), cols], p_sem.at[0, m])
            wait_bytes(xv.at[pl.ds(0, 32), cols], f_sem.at[0, m])

        return 0

    lax.fori_loop(0, UNITS, left, 0)
    wait_bytes(rowinfo.at[0], row_sem.at[2])
    for j in range(4):
        wait_bytes(half.at[1, :, pl.ds(0, ROWS)], half_sem.at[0, j])
    for g in range(GROUPS):
        wait_bytes(final.at[core, :, pl.ds(g * GROUP, GROUP)], final_sem.at[0, g])
    for (_, in1, _, in2), sems in ((stat_bufs, stat_sem), (mass_bufs, mass_sem), (kept_bufs, kept_sem)):
        for trip in range(in1.shape[0]):
            wait_bytes(in1.at[trip], sems.at[0, trip])
            wait_bytes(in2.at[trip], sems.at[2, trip])


def slots(count, height):
    f32 = jnp.float32
    return [
        pltpu.VMEM((count, height, GROUP), f32),
        pltpu.VMEM((count, 15, height, GROUP), f32),
        pltpu.VMEM((count, height, GROUP), f32),
        pltpu.VMEM((count, 3, height, GROUP), f32),
    ]


def on_device(latent_vectors, unembedding_matrix, softmax_divisor, top_probability_quota):
    weights = unembedding_matrix.T
    vocab, depth = weights.shape
    batch = 8 * ROWS
    f32 = jnp.float32
    dma = pltpu.SemaphoreType.DMA
    vmem = pl.BlockSpec(memory_space=pltpu.VMEM)
    hbm = pl.BlockSpec(memory_space=pl.ANY)
    out, scale = pl.pallas_call(
        kernel,
        out_shape=[jax.ShapeDtypeStruct((vocab, batch), f32), jax.ShapeDtypeStruct((1, batch), f32)],
        in_specs=[hbm, hbm, vmem, vmem],
        out_specs=[vmem, vmem],
        scratch_shapes=[
            pltpu.VMEM((batch, depth), jnp.bfloat16),
            pltpu.VMEM((vocab, depth), jnp.bfloat16),
            pltpu.VMEM((vocab, batch), f32),
            pltpu.VMEM((2, vocab, HALF), f32),
            pltpu.VMEM((2, vocab, HALF), f32),
            pltpu.VMEM((2, 4, 2, ROWS), f32),
            pltpu.VMEM((2, 2, HALF), f32),
            pltpu.VMEM((2, 1, HALF), f32),
            slots(GROUPS, 2),
            slots(GROUPS * BISECT_PASSES, 4),
            slots(GROUPS, 1),
            pltpu.SemaphoreType.REGULAR,
            dma((CHUNKS + 1,)),
            dma((4,)),
            dma((2, UNITS)),
            dma((2, UNITS)),
            dma((2, UNITS)),
            dma((2, UNITS)),
            dma((2, 4)),
            dma((2, GROUPS + 1)),
            dma((4, GROUPS)),
            dma((4, GROUPS * BISECT_PASSES)),
            dma((4, GROUPS)),
        ],
        compiler_params=pltpu.CompilerParams(
            collective_id=0, has_side_effects=True, vmem_limit_bytes=58 * 1024 * 1024
        ),
        cost_estimate=pl.CostEstimate(
            flops=2 * vocab * depth * batch, bytes_accessed=2 * depth * (vocab + batch), transcendentals=20 * vocab * batch
        ),
    )(latent_vectors, weights, softmax_divisor[None, :], top_probability_quota[None, :])
    return (out * scale).T


def solution(mesh):
    placed = (P("dp", None), P(None, ("dp", "vocab")), P("dp"), P("dp"))
    return jax.shard_map(
        on_device, mesh=mesh, in_specs=placed, out_specs=P(None, ("dp", "vocab")), check_vma=False
    )
```

```python
import functools

import jax
import jax.numpy as jnp
from jax import lax
from jax.experimental import pallas as pl
from jax.experimental.pallas import tpu as pltpu
from jax.sharding import PartitionSpec as P

MESH = pl.DeviceIdType.MESH
BISECT_PASSES = 4
PROBES = 4
soft_width = 0.25
sharpness = 0.02
initial_level = -16.0
first_spacing = 4.0

ROWS = 128
HALF = 512
GROUP = 128
GROUPS = 4
OUT_ROWS = 512
STRIP = 336
CHUNKS = 4
UNITS = 4 * CHUNKS
LAG_FORWARD = 2
LAG_SHARE = 4
LAG_MULTIPLY = 5
EARLY = 1
NT = (((1,), (1,)), ((), ()))


def wait_bytes(ref, sem):
    pltpu.make_async_copy(ref, ref, sem).wait()


def places():
    dp, vo = lax.axis_index("dp"), lax.axis_index("vocab")
    plane = [(dp, lax.rem(vo + d, 16)) for d in range(1, 16)]
    column = [(lax.rem(dp + 2 * d, 8), vo) for d in range(1, 4)]
    sibling = (dp + 1 - 2 * lax.rem(dp, 2), vo)
    x_at, z_at = lax.div(vo, 4), lax.rem(vo, 4)
    line_z = [(dp, x_at * 4 + lax.rem(z_at + e, 4)) for e in range(1, 4)]
    line_x = [(dp, lax.rem(x_at + e, 4) * 4 + z_at) for e in range(1, 4)]
    return dp, x_at, z_at, plane, column, sibling, line_z, line_x


def send(src, dst, send_sem, recv_sem, device):
    copy = pltpu.make_async_remote_copy(
        src_ref=src, dst_ref=dst, send_sem=send_sem, recv_sem=recv_sem, device_id=device, device_id_type=MESH
    )
    copy.start()
    return copy


def fold(fn, init, vocab):
    def step(t, carry):
        base = pl.multiple_of(t * STRIP, 8)
        for i in range(STRIP // 8):
            carry = fn(carry, pl.ds(base + 8 * i, 8))
        return carry

    return lax.fori_loop(0, vocab // STRIP, step, init)


def exchange(value, join, trip, plane, column, bufs, sems):
    out1, in1, out2, in2 = bufs
    out1[trip] = value
    for d, device in enumerate(plane):
        send(out1.at[trip], in1.at[trip, d], sems.at[0, trip], sems.at[1, trip], device)
    yield
    wait_bytes(in1.at[trip], sems.at[1, trip])
    value = join([value] + [in1[trip, d] for d in range(15)])
    out2[trip] = value
    for d, device in enumerate(column):
        send(out2.at[trip], in2.at[trip, d], sems.at[2, trip], sems.at[3, trip], device)
    yield
    wait_bytes(in2.at[trip], sems.at[3, trip])
    return join([value] + [in2[trip, d] for d in range(3)])


def total_sum(parts):
    while len(parts) > 1:
        parts = [a + b for a, b in zip(parts[::2], parts[1::2])] + parts[len(parts) & ~1 :]
    return parts[0]


def joined_stats(parts):
    peak = functools.reduce(jnp.maximum, [p[0:1] for p in parts])
    summed = total_sum([p[1:2] * jnp.exp(0.5 * (p[0:1] - peak)) for p in parts])
    return jnp.concatenate([peak, summed], axis=0)


def kernel(
    x_ref, w_ref, div_ref, quota_ref, out_ref, scale_ref,
    xv, wv, logit, weighed, half, expo, rowinfo, final, scale,
    stat_bufs, mass_bufs, kept_bufs,
    plane_sem, load_sem, row_sem, y_sem, p_sem, f_sem, c_sem, half_sem, final_sem, out_sem, stat_sem, mass_sem, kept_sem,
):
    dp, x_at, z_at, plane, column, sibling, line_z, line_x = places()
    y_at = lax.div(dp, 2)
    core = lax.rem(dp, 2)
    vocab = w_ref.shape[0]
    depth = w_ref.shape[1]
    chunk = depth // CHUNKS
    load_x = pltpu.make_async_copy(x_ref, xv.at[pl.ds(pl.multiple_of(dp * ROWS, ROWS), ROWS)], load_sem.at[CHUNKS])
    load_x.start()
    load_w = []
    for k in range(CHUNKS):
        cols = pl.ds(k * chunk, chunk)
        load_w.append(pltpu.make_async_copy(w_ref.at[:, cols], wv.at[:, cols], load_sem.at[k]))
        load_w[k].start()

    barrier = pltpu.get_barrier_semaphore()
    greeted = line_z + line_x + column + [sibling]
    for device in greeted:
        pl.semaphore_signal(barrier, inc=1, device_id=device, device_id_type=MESH)
    rowinfo[core, y_at] = jnp.concatenate([2.0 / div_ref[...], quota_ref[...].astype(jnp.float32) / 100.0], axis=0)
    pl.semaphore_wait(barrier, len(greeted))

    for device in line_x:
        pl.semaphore_signal(plane_sem, inc=1, device_id=device, device_id_type=MESH)
    for device in column:
        send(rowinfo.at[core, y_at], rowinfo.at[core, y_at], row_sem.at[0], row_sem.at[1], device)

    first_row = pl.multiple_of(dp * ROWS, ROWS)

    def unit(m):
        i = m - CHUNKS
        near = i < 2 * CHUNKS
        offset = jnp.where(i < 0, 0, jnp.where(near, 1 + 2 * lax.rem(i, 2), 2))
        k = jnp.where(i < 0, m, jnp.where(near, lax.div(i, 2), i - 2 * CHUNKS))
        return offset, pl.ds(pl.multiple_of(k * chunk, chunk), chunk), k

    def pieces(block):
        base = block * ROWS
        return (
            pl.ds(pl.multiple_of(base + 16 * z_at, 16), 16),
            pl.ds(pl.multiple_of(base + 64 + 16 * x_at, 16), 16),
        )

    def spread(m, _):
        offset, cols, _ = unit(m)
        target = (lax.rem(2 * (y_at + 4 - offset) + core, 8), column[0][1])
        for local, there in zip(pieces(0), pieces(dp)):
            send(x_ref.at[local, cols], xv.at[there, cols], y_sem.at[0, m], y_sem.at[1, m], target)
        return 0

    def share_own(m, _):
        _, cols, _ = unit(m)
        send(x_ref.at[:, cols], xv.at[pl.ds(first_row, ROWS), cols], c_sem.at[0, m], c_sem.at[1, m], sibling)
        return 0

    def source_block(offset):
        return lax.rem(2 * (y_at + offset) + core, 8)

    def pass_on(m):
        offset, cols, _ = unit(m)
        wait_bytes(xv.at[pl.ds(0, 32), cols], y_sem.at[1, m])
        for rows, line in zip(pieces(source_block(offset)), (line_z, line_x)):
            for device in (line[0], line[2]):
                send(xv.at[rows, cols], xv.at[rows, cols], p_sem.at[0, m], p_sem.at[1, m], device)

    def forward(m):
        offset, cols, k = unit(m)
        wait_bytes(xv.at[pl.ds(0, 64), cols], p_sem.at[1, m])
        base = source_block(offset) * ROWS
        for at, shift, line in ((z_at, 0, line_z), (x_at, 64, line_x)):
            for part, (step, device) in enumerate(((3, line[0]), (1, line[2]))):
                rows = pl.ds(pl.multiple_of(base + shift + 16 * lax.rem(at + step, 4), 16), 16)
                cols = pl.ds(pl.multiple_of(k * chunk + part * (chunk // 2), chunk // 2), chunk // 2)
                send(xv.at[rows, cols], xv.at[rows, cols], f_sem.at[0, m], f_sem.at[1, m], device)

    def share(m):
        offset, cols, _ = unit(m)
        wait_bytes(xv.at[pl.ds(0, 32), cols], f_sem.at[1, m])
        rows = pl.ds(pl.multiple_of(source_block(offset) * ROWS, ROWS), ROWS)
        send(xv.at[rows, cols], xv.at[rows, cols], c_sem.at[0, m], c_sem.at[1, m], sibling)

    def multiply(m):
        offset, cols, k = unit(m)
        plane_at = lax.rem(y_at + offset, 4)
        rows = pl.ds(pl.multiple_of(plane_at * 2 * ROWS, 2 * ROWS), 2 * ROWS)
        wait_bytes(xv.at[pl.ds(0, ROWS), cols], c_sem.at[1, m])
        logit[:, rows] += lax.dot_general(wv[:, cols], xv[rows, cols], NT, preferred_element_type=jnp.float32)

        @pl.when(k == CHUNKS - 1)
        def _():
            block = 2 * plane_at + 1 - core
            cols = pl.ds(pl.multiple_of(block * ROWS, ROWS), ROWS)
            there = pl.ds(pl.multiple_of(plane_at * ROWS, ROWS), ROWS)
            logit[:, cols] = logit[:, cols] * rowinfo[1 - core, plane_at, 0:1]
            send(logit.at[:, cols], half.at[1, :, there], half_sem.at[0, plane_at], half_sem.at[1, plane_at], sibling)
            block = 2 * plane_at + core
            cols = pl.ds(pl.multiple_of(block * ROWS, ROWS), ROWS)
            value = logit[:, cols] * rowinfo[core, plane_at, 0:1]
            logit[:, cols] = value
            half[0, :, there] = value

    lax.fori_loop(0, CHUNKS, share_own, 0)
    lax.fori_loop(CHUNKS, UNITS, spread, 0)
    logit[...] = jnp.zeros_like(logit)
    load_x.wait()
    for m in range(EARLY):
        load_w[m].wait()
        multiply(m)
    wait_bytes(rowinfo.at[0, pl.ds(0, 3)], row_sem.at[1])
    wait_bytes(rowinfo.at[0, pl.ds(0, 3)], row_sem.at[0])
    send(rowinfo.at[core], rowinfo.at[core], row_sem.at[2], row_sem.at[3], sibling)

    def step(t, _):
        @pl.when(t < UNITS)
        def _():
            pass_on(t)

        @pl.when((t >= CHUNKS + LAG_FORWARD) & (t < UNITS + LAG_FORWARD))
        def _():
            forward(t - LAG_FORWARD)

        @pl.when((t >= CHUNKS + LAG_SHARE) & (t < UNITS + LAG_SHARE))
        def _():
            share(t - LAG_SHARE)

        m = t - LAG_MULTIPLY

        @pl.when(m == EARLY)
        def _():
            wait_bytes(rowinfo.at[0], row_sem.at[3])

        @pl.when((m >= EARLY) & (m < CHUNKS))
        def _():
            wait_bytes(wv.at[:, pl.ds(0, chunk)], load_sem.at[m])

        @pl.when(m >= EARLY)
        def _():
            multiply(m)

        return 0

    lax.fori_loop(CHUNKS, UNITS + LAG_MULTIPLY, step, 0)
    pl.semaphore_wait(plane_sem, 3)
    level = jnp.concatenate([rowinfo[core, j, 1:2] for j in range(4)], axis=1)
    for j in range(4):
        wait_bytes(half.at[1, :, pl.ds(0, ROWS)], half_sem.at[1, j])

    tail = pl.ds(vocab // 8 * 8, vocab % 8)

    def follow(g):
        lanes = slice(g * GROUP, (g + 1) * GROUP)

        peak = jnp.full((8, GROUP), -3e38, jnp.float32)
        for v in range(2):
            peak = fold(lambda c, r: jnp.maximum(c, half[v, r, lanes]), peak, vocab)
        peak = jnp.max(peak, axis=0, keepdims=True)
        for v in range(2):
            peak = jnp.maximum(peak, jnp.max(half[v, tail, lanes], axis=0, keepdims=True))
        own_sum = jnp.zeros((8, GROUP), jnp.float32)
        wide = jnp.broadcast_to(peak, (8, GROUP))
        tail_sum = jnp.zeros((1, GROUP), jnp.float32)
        for v in range(2):

            def add_exp(carry, r):
                e = jnp.exp(0.5 * (half[v, r, lanes] - wide))
                expo[v, r, lanes] = e
                return carry + e

            own_sum = fold(add_exp, own_sum, vocab)
            e = jnp.exp(0.5 * (half[v, tail, lanes] - peak))
            expo[v, tail, lanes] = e
            tail_sum = tail_sum + jnp.sum(e, axis=0, keepdims=True)
        own_sum = jnp.sum(own_sum, axis=0, keepdims=True) + tail_sum
        stats = yield from exchange(
            jnp.concatenate([peak, own_sum], axis=0), joined_stats, g, plane, column, stat_bufs, stat_sem
        )
        top, total = stats[0:1], stats[1:2]
        share = 0.5 * jnp.exp(0.5 * (peak - top)) / total

        def masses(cuts):
            n = len(cuts)
            wides = [jnp.broadcast_to(c, (8, GROUP)) for c in cuts]
            sums = tuple(jnp.zeros((8, GROUP), jnp.float32) for _ in cuts)
            rest = [jnp.zeros((1, GROUP), jnp.float32) for _ in cuts]
            for v in range(2):

                def add(carry, r):
                    l, e = half[v, r, lanes], expo[v, r, lanes]
                    return tuple(carry[k] + e * jnp.tanh(l - wides[k]) for k in range(n))

                sums = fold(add, sums, vocab)
                l, e = half[v, tail, lanes], expo[v, tail, lanes]
                rest = [rest[k] + jnp.sum(e * jnp.tanh(l - cuts[k]), axis=0, keepdims=True) for k in range(n)]
            parts = [share * (own_sum + jnp.sum(sums[k], axis=0, keepdims=True) + rest[k]) for k in range(n)]
            return jnp.concatenate(parts, axis=0)

        lower, spacing = jnp.full((1, GROUP), initial_level, jnp.float32), first_spacing
        for r in range(BISECT_PASSES):
            parts = masses([top + 2.0 * (lower + spacing * (k + 1)) for k in range(PROBES)])
            mass = yield from exchange(
                parts, total_sum, r * GROUPS + g, plane, column, mass_bufs, mass_sem
            )
            passed = jnp.sum(jax.nn.sigmoid((mass - level[:, lanes]) / sharpness), axis=0, keepdims=True)
            estimate = lower + spacing * passed
            spacing = spacing / 2.0
            lower = estimate - spacing
        cut = top + 2.0 * (lower + 2.0 * spacing)
        final[core, 0:1, lanes] = top
        final[core, 1:2, lanes] = cut
        here = final.at[core, :, pl.ds(g * GROUP, GROUP)]
        send(here, here, final_sem.at[0, g], final_sem.at[1, g], sibling)
        kept = yield from exchange(masses([cut]), total_sum, g, plane, column, kept_bufs, kept_sem)
        scale[core, 0:1, lanes] = 1.0 / (total * kept)

    def weigh(h, g):
        for j in range(g * GROUP // ROWS, (g + 1) * GROUP // ROWS):
            lanes = slice(j * ROWS, (j + 1) * ROWS)
            cols = pl.ds(pl.multiple_of((2 * j + h) * ROWS, ROWS), ROWS)
            top, cut = final[h, 0:1, lanes], final[h, 1:2, lanes]
            value = logit[:, cols]
            weighed[:, cols] = jnp.exp(0.5 * (value - top)) * (0.5 + 0.5 * jnp.tanh(value - cut))
            pltpu.make_async_copy(weighed.at[:, cols], out_ref.at[:, cols], out_sem.at[h, j]).start()

    rows_of = [follow(g) for g in range(GROUPS)]
    for _ in range(BISECT_PASSES + 1):
        for part in range(2):
            for rows in rows_of:
                next(rows)
    for rows in rows_of:
        next(rows)
    for g in range(GROUPS):
        weigh(core, g)
    for g in range(GROUPS):
        wait_bytes(final.at[core, :, pl.ds(g * GROUP, GROUP)], final_sem.at[1, g])
        weigh(1 - core, g)
    for rows in rows_of:
        next(rows)
    for rows in rows_of:
        next(rows, None)
    swap = send(scale.at[core], scale.at[core], final_sem.at[0, GROUPS], final_sem.at[1, GROUPS], sibling)
    swap.wait()
    for block in range(8):
        lanes = slice(block // 2 * ROWS, (block // 2 + 1) * ROWS)
        scale_ref[:, block * ROWS : (block + 1) * ROWS] = scale[block % 2, :, lanes]

    for h in range(2):
        for j in range(4):
            cols = pl.ds((2 * j + h) * ROWS, ROWS)
            pltpu.make_async_copy(weighed.at[:, cols], out_ref.at[:, cols], out_sem.at[h, j]).wait()

    def left(m, _):
        cols = pl.ds(0, chunk)
        wait_bytes(xv.at[pl.ds(0, ROWS), cols], c_sem.at[0, m])

        @pl.when(m >= CHUNKS)
        def _():
            wait_bytes(xv.at[pl.ds(0, 32), cols], y_sem.at[0, m])
            wait_bytes(xv.at[pl.ds(0, 64), cols], p_sem.at[0, m])
            wait_bytes(xv.at[pl.ds(0, 32), cols], f_sem.at[0, m])

        return 0

    lax.fori_loop(0, UNITS, left, 0)
    wait_bytes(rowinfo.at[0], row_sem.at[2])
    for j in range(4):
        wait_bytes(half.at[1, :, pl.ds(0, ROWS)], half_sem.at[0, j])
    for g in range(GROUPS):
        wait_bytes(final.at[core, :, pl.ds(g * GROUP, GROUP)], final_sem.at[0, g])
    for (_, in1, _, in2), sems in ((stat_bufs, stat_sem), (mass_bufs, mass_sem), (kept_bufs, kept_sem)):
        for trip in range(in1.shape[0]):
            wait_bytes(in1.at[trip], sems.at[0, trip])
            wait_bytes(in2.at[trip], sems.at[2, trip])


def rescale(weight_ref, scale_ref, out_ref):
    out_ref[...] = weight_ref[...] * scale_ref[...]


def slots(count, height):
    f32 = jnp.float32
    return [
        pltpu.VMEM((count, height, GROUP), f32),
        pltpu.VMEM((count, 15, height, GROUP), f32),
        pltpu.VMEM((count, height, GROUP), f32),
        pltpu.VMEM((count, 3, height, GROUP), f32),
    ]


def on_device(latent_vectors, unembedding_matrix, softmax_divisor, top_probability_quota):
    weights = unembedding_matrix.T
    vocab, depth = weights.shape
    batch = 8 * ROWS
    f32 = jnp.float32
    dma = pltpu.SemaphoreType.DMA
    vmem = pl.BlockSpec(memory_space=pltpu.VMEM)
    hbm = pl.BlockSpec(memory_space=pl.ANY)
    out, scale = pl.pallas_call(
        kernel,
        out_shape=[jax.ShapeDtypeStruct((vocab, batch), f32), jax.ShapeDtypeStruct((1, batch), f32)],
        in_specs=[hbm, hbm, vmem, vmem],
        out_specs=[hbm, vmem],
        scratch_shapes=[
            pltpu.VMEM((batch, depth), jnp.bfloat16),
            pltpu.VMEM((vocab, depth), jnp.bfloat16),
            pltpu.VMEM((vocab, batch), f32),
            pltpu.VMEM((vocab, batch), f32),
            pltpu.VMEM((2, vocab, HALF), f32),
            pltpu.VMEM((2, vocab, HALF), f32),
            pltpu.VMEM((2, 4, 2, ROWS), f32),
            pltpu.VMEM((2, 2, HALF), f32),
            pltpu.VMEM((2, 1, HALF), f32),
            slots(GROUPS, 2),
            slots(GROUPS * BISECT_PASSES, 4),
            slots(GROUPS, 1),
            pltpu.SemaphoreType.REGULAR,
            dma((CHUNKS + 1,)),
            dma((4,)),
            dma((2, UNITS)),
            dma((2, UNITS)),
            dma((2, UNITS)),
            dma((2, UNITS)),
            dma((2, 4)),
            dma((2, GROUPS + 1)),
            dma((2, 4)),
            dma((4, GROUPS)),
            dma((4, GROUPS * BISECT_PASSES)),
            dma((4, GROUPS)),
        ],
        compiler_params=pltpu.CompilerParams(
            collective_id=0, has_side_effects=True, vmem_limit_bytes=58 * 1024 * 1024
        ),
        cost_estimate=pl.CostEstimate(
            flops=2 * vocab * depth * batch, bytes_accessed=2 * depth * (vocab + batch), transcendentals=20 * vocab * batch
        ),
    )(latent_vectors, weights, softmax_divisor[None, :], top_probability_quota[None, :])
    block = pl.BlockSpec((OUT_ROWS, batch), lambda i: (i, 0))
    return pl.pallas_call(
        rescale,
        grid=(pl.cdiv(vocab, OUT_ROWS),),
        out_shape=jax.ShapeDtypeStruct((vocab, batch), f32),
        in_specs=[block, pl.BlockSpec((1, batch), lambda i: (0, 0))],
        out_specs=block,
    )(out, scale).T


def solution(mesh):
    placed = (P("dp", None), P(None, ("dp", "vocab")), P("dp"), P("dp"))
    return jax.shard_map(
        on_device, mesh=mesh, in_specs=placed, out_specs=P(None, ("dp", "vocab")), check_vma=False
    )
```

```python
import functools

import jax
import jax.numpy as jnp
from jax import lax
from jax.experimental import pallas as pl
from jax.experimental.pallas import tpu as pltpu
from jax.sharding import PartitionSpec as P

MESH = pl.DeviceIdType.MESH
BISECT_PASSES = 4
PROBES = 4
soft_width = 0.25
sharpness = 0.02
initial_level = -16.0
first_spacing = 4.0

ROWS = 128
HALF = 512
GROUP = 128
GROUPS = 4
OUT_ROWS = 512
STRIP = 336
CHUNKS = 4
UNITS = 4 * CHUNKS
LAG_FORWARD = 2
LAG_SHARE = 4
LAG_MULTIPLY = 5
EARLY = 1
NT = (((1,), (1,)), ((), ()))


def wait_bytes(ref, sem):
    pltpu.make_async_copy(ref, ref, sem).wait()


def places():
    dp, vo = lax.axis_index("dp"), lax.axis_index("vocab")
    column = [(lax.rem(dp + 2 * d, 8), vo) for d in (2, 1, 3)]
    sibling = (dp + 1 - 2 * lax.rem(dp, 2), vo)
    x_at, z_at = lax.div(vo, 4), lax.rem(vo, 4)
    steps = sorted(((a, e) for a in range(4) for e in range(4) if a or e), key=lambda s: abs(s[0] - 2) + abs(s[1] - 2))
    plane = [(dp, lax.rem(x_at + a, 4) * 4 + lax.rem(z_at + e, 4)) for a, e in steps]
    line_z = [(dp, x_at * 4 + lax.rem(z_at + e, 4)) for e in range(1, 4)]
    line_x = [(dp, lax.rem(x_at + e, 4) * 4 + z_at) for e in range(1, 4)]
    return dp, x_at, z_at, plane, column, sibling, line_z, line_x


def send(src, dst, send_sem, recv_sem, device):
    copy = pltpu.make_async_remote_copy(
        src_ref=src, dst_ref=dst, send_sem=send_sem, recv_sem=recv_sem, device_id=device, device_id_type=MESH
    )
    copy.start()
    return copy


def fold(fn, init, vocab):
    def step(t, carry):
        base = pl.multiple_of(t * STRIP, 8)
        for i in range(STRIP // 8):
            carry = fn(carry, pl.ds(base + 8 * i, 8))
        return carry

    return lax.fori_loop(0, vocab // STRIP, step, init)


def exchange(value, join, trip, plane, column, bufs, sems):
    out1, in1, out2, in2 = bufs
    out1[trip] = value
    for d, device in enumerate(plane):
        send(out1.at[trip], in1.at[trip, d], sems.at[0, trip], sems.at[1, trip], device)
    yield
    wait_bytes(in1.at[trip], sems.at[1, trip])
    value = join([value] + [in1[trip, d] for d in range(15)])
    out2[trip] = value
    for d, device in enumerate(column):
        send(out2.at[trip], in2.at[trip, d], sems.at[2, trip], sems.at[3, trip], device)
    yield
    wait_bytes(in2.at[trip], sems.at[3, trip])
    return join([value] + [in2[trip, d] for d in range(3)])


def total_sum(parts):
    while len(parts) > 1:
        parts = [a + b for a, b in zip(parts[::2], parts[1::2])] + parts[len(parts) & ~1 :]
    return parts[0]


def joined_stats(parts):
    peak = functools.reduce(jnp.maximum, [p[0:1] for p in parts])
    summed = total_sum([p[1:2] * jnp.exp(0.5 * (p[0:1] - peak)) for p in parts])
    return jnp.concatenate([peak, summed], axis=0)


def kernel(
    x_ref, w_ref, div_ref, quota_ref, out_ref, scale_ref,
    xv, wv, logit, weighed, half, expo, rowinfo, final, scale,
    stat_bufs, mass_bufs, kept_bufs,
    plane_sem, load_sem, row_sem, y_sem, p_sem, f_sem, c_sem, half_sem, final_sem, out_sem, stat_sem, mass_sem, kept_sem,
):
    dp, x_at, z_at, plane, column, sibling, line_z, line_x = places()
    y_at = lax.div(dp, 2)
    core = lax.rem(dp, 2)
    vocab = w_ref.shape[0]
    depth = w_ref.shape[1]
    chunk = depth // CHUNKS
    load_x = pltpu.make_async_copy(x_ref, xv.at[pl.ds(pl.multiple_of(dp * ROWS, ROWS), ROWS)], load_sem.at[CHUNKS])
    load_x.start()
    load_w = []
    for k in range(CHUNKS):
        cols = pl.ds(k * chunk, chunk)
        load_w.append(pltpu.make_async_copy(w_ref.at[:, cols], wv.at[:, cols], load_sem.at[k]))
        load_w[k].start()

    barrier = pltpu.get_barrier_semaphore()
    greeted = line_z + line_x + column + [sibling]
    for device in greeted:
        pl.semaphore_signal(barrier, inc=1, device_id=device, device_id_type=MESH)
    rowinfo[core, y_at] = jnp.concatenate([2.0 / div_ref[...], quota_ref[...].astype(jnp.float32) / 100.0], axis=0)
    pl.semaphore_wait(barrier, len(greeted))

    for device in line_x:
        pl.semaphore_signal(plane_sem, inc=1, device_id=device, device_id_type=MESH)
    for device in column:
        send(rowinfo.at[core, y_at], rowinfo.at[core, y_at], row_sem.at[0], row_sem.at[1], device)

    first_row = pl.multiple_of(dp * ROWS, ROWS)

    def unit(m):
        i = m - CHUNKS
        near = i < 2 * CHUNKS
        offset = jnp.where(i < 0, 0, jnp.where(near, 1 + 2 * lax.rem(i, 2), 2))
        k = jnp.where(i < 0, m, jnp.where(near, lax.div(i, 2), i - 2 * CHUNKS))
        return offset, pl.ds(pl.multiple_of(k * chunk, chunk), chunk), k

    def pieces(block):
        base = block * ROWS
        return (
            pl.ds(pl.multiple_of(base + 16 * z_at, 16), 16),
            pl.ds(pl.multiple_of(base + 64 + 16 * x_at, 16), 16),
        )

    def spread(m, _):
        offset, cols, _ = unit(m)
        target = (lax.rem(2 * (y_at + 4 - offset) + core, 8), column[0][1])
        for local, there in zip(pieces(0), pieces(dp)):
            send(x_ref.at[local, cols], xv.at[there, cols], y_sem.at[0, m], y_sem.at[1, m], target)
        return 0

    def share_own(m, _):
        _, cols, _ = unit(m)
        send(x_ref.at[:, cols], xv.at[pl.ds(first_row, ROWS), cols], c_sem.at[0, m], c_sem.at[1, m], sibling)
        return 0

    def source_block(offset):
        return lax.rem(2 * (y_at + offset) + core, 8)

    def pass_on(m):
        offset, cols, _ = unit(m)
        wait_bytes(xv.at[pl.ds(0, 32), cols], y_sem.at[1, m])
        for rows, line in zip(pieces(source_block(offset)), (line_z, line_x)):
            for device in (line[0], line[2]):
                send(xv.at[rows, cols], xv.at[rows, cols], p_sem.at[0, m], p_sem.at[1, m], device)

    def forward(m):
        offset, cols, k = unit(m)
        wait_bytes(xv.at[pl.ds(0, 64), cols], p_sem.at[1, m])
        base = source_block(offset) * ROWS
        for at, shift, line in ((z_at, 0, line_z), (x_at, 64, line_x)):
            for part, (step, device) in enumerate(((3, line[0]), (1, line[2]))):
                rows = pl.ds(pl.multiple_of(base + shift + 16 * lax.rem(at + step, 4), 16), 16)
                cols = pl.ds(pl.multiple_of(k * chunk + part * (chunk // 2), chunk // 2), chunk // 2)
                send(xv.at[rows, cols], xv.at[rows, cols], f_sem.at[0, m], f_sem.at[1, m], device)

    def share(m):
        offset, cols, _ = unit(m)
        wait_bytes(xv.at[pl.ds(0, 32), cols], f_sem.at[1, m])
        rows = pl.ds(pl.multiple_of(source_block(offset) * ROWS, ROWS), ROWS)
        send(xv.at[rows, cols], xv.at[rows, cols], c_sem.at[0, m], c_sem.at[1, m], sibling)

    def multiply(m):
        offset, cols, k = unit(m)
        plane_at = lax.rem(y_at + offset, 4)
        rows = pl.ds(pl.multiple_of(plane_at * 2 * ROWS, 2 * ROWS), 2 * ROWS)
        wait_bytes(xv.at[pl.ds(0, ROWS), cols], c_sem.at[1, m])
        logit[:, rows] += lax.dot_general(wv[:, cols], xv[rows, cols], NT, preferred_element_type=jnp.float32)

        @pl.when(k == CHUNKS - 1)
        def _():
            block = 2 * plane_at + 1 - core
            cols = pl.ds(pl.multiple_of(block * ROWS, ROWS), ROWS)
            there = pl.ds(pl.multiple_of(plane_at * ROWS, ROWS), ROWS)
            logit[:, cols] = logit[:, cols] * rowinfo[1 - core, plane_at, 0:1]
            send(logit.at[:, cols], half.at[1, :, there], half_sem.at[0, plane_at], half_sem.at[1, plane_at], sibling)
            block = 2 * plane_at + core
            cols = pl.ds(pl.multiple_of(block * ROWS, ROWS), ROWS)
            value = logit[:, cols] * rowinfo[core, plane_at, 0:1]
            logit[:, cols] = value
            half[0, :, there] = value

    lax.fori_loop(0, CHUNKS, share_own, 0)
    lax.fori_loop(CHUNKS, UNITS, spread, 0)
    logit[...] = jnp.zeros_like(logit)
    load_x.wait()
    for m in range(EARLY):
        load_w[m].wait()
        multiply(m)
    wait_bytes(rowinfo.at[0, pl.ds(0, 3)], row_sem.at[1])
    wait_bytes(rowinfo.at[0, pl.ds(0, 3)], row_sem.at[0])
    send(rowinfo.at[core], rowinfo.at[core], row_sem.at[2], row_sem.at[3], sibling)

    def step(t, _):
        @pl.when(t < UNITS)
        def _():
            pass_on(t)

        @pl.when((t >= CHUNKS + LAG_FORWARD) & (t < UNITS + LAG_FORWARD))
        def _():
            forward(t - LAG_FORWARD)

        @pl.when((t >= CHUNKS + LAG_SHARE) & (t < UNITS + LAG_SHARE))
        def _():
            share(t - LAG_SHARE)

        m = t - LAG_MULTIPLY

        @pl.when(m == EARLY)
        def _():
            wait_bytes(rowinfo.at[0], row_sem.at[3])

        @pl.when((m >= EARLY) & (m < CHUNKS))
        def _():
            wait_bytes(wv.at[:, pl.ds(0, chunk)], load_sem.at[m])

        @pl.when(m >= EARLY)
        def _():
            multiply(m)

        return 0

    lax.fori_loop(CHUNKS, UNITS + LAG_MULTIPLY, step, 0)
    pl.semaphore_wait(plane_sem, 3)
    level = jnp.concatenate([rowinfo[core, j, 1:2] for j in range(4)], axis=1)
    for j in range(4):
        wait_bytes(half.at[1, :, pl.ds(0, ROWS)], half_sem.at[1, j])

    tail = pl.ds(vocab // 8 * 8, vocab % 8)

    def follow(g):
        lanes = slice(g * GROUP, (g + 1) * GROUP)

        peak = jnp.full((8, GROUP), -3e38, jnp.float32)
        for v in range(2):
            peak = fold(lambda c, r: jnp.maximum(c, half[v, r, lanes]), peak, vocab)
        peak = jnp.max(peak, axis=0, keepdims=True)
        for v in range(2):
            peak = jnp.maximum(peak, jnp.max(half[v, tail, lanes], axis=0, keepdims=True))
        own_sum = jnp.zeros((8, GROUP), jnp.float32)
        wide = jnp.broadcast_to(peak, (8, GROUP))
        tail_sum = jnp.zeros((1, GROUP), jnp.float32)
        for v in range(2):

            def add_exp(carry, r):
                e = jnp.exp(0.5 * (half[v, r, lanes] - wide))
                expo[v, r, lanes] = e
                return carry + e

            own_sum = fold(add_exp, own_sum, vocab)
            e = jnp.exp(0.5 * (half[v, tail, lanes] - peak))
            expo[v, tail, lanes] = e
            tail_sum = tail_sum + jnp.sum(e, axis=0, keepdims=True)
        own_sum = jnp.sum(own_sum, axis=0, keepdims=True) + tail_sum
        stats = yield from exchange(
            jnp.concatenate([peak, own_sum], axis=0), joined_stats, g, plane, column, stat_bufs, stat_sem
        )
        top, total = stats[0:1], stats[1:2]
        share = 0.5 * jnp.exp(0.5 * (peak - top)) / total

        def masses(cuts):
            n = len(cuts)
            wides = [jnp.broadcast_to(c, (8, GROUP)) for c in cuts]
            sums = tuple(jnp.zeros((8, GROUP), jnp.float32) for _ in cuts)
            rest = [jnp.zeros((1, GROUP), jnp.float32) for _ in cuts]
            for v in range(2):

                def add(carry, r):
                    l, e = half[v, r, lanes], expo[v, r, lanes]
                    return tuple(carry[k] + e * jnp.tanh(l - wides[k]) for k in range(n))

                sums = fold(add, sums, vocab)
                l, e = half[v, tail, lanes], expo[v, tail, lanes]
                rest = [rest[k] + jnp.sum(e * jnp.tanh(l - cuts[k]), axis=0, keepdims=True) for k in range(n)]
            parts = [share * (own_sum + jnp.sum(sums[k], axis=0, keepdims=True) + rest[k]) for k in range(n)]
            return jnp.concatenate(parts, axis=0)

        lower, spacing = jnp.full((1, GROUP), initial_level, jnp.float32), first_spacing
        for r in range(BISECT_PASSES):
            parts = masses([top + 2.0 * (lower + spacing * (k + 1)) for k in range(PROBES)])
            mass = yield from exchange(
                parts, total_sum, r * GROUPS + g, plane, column, mass_bufs, mass_sem
            )
            passed = jnp.sum(jax.nn.sigmoid((mass - level[:, lanes]) / sharpness), axis=0, keepdims=True)
            estimate = lower + spacing * passed
            spacing = spacing / 2.0
            lower = estimate - spacing
        cut = top + 2.0 * (lower + 2.0 * spacing)
        final[core, 0:1, lanes] = top
        final[core, 1:2, lanes] = cut
        here = final.at[core, :, pl.ds(g * GROUP, GROUP)]
        send(here, here, final_sem.at[0, g], final_sem.at[1, g], sibling)
        kept = yield from exchange(masses([cut]), total_sum, g, plane, column, kept_bufs, kept_sem)
        scale[core, 0:1, lanes] = 1.0 / (total * kept)

    def weigh(h, g):
        for j in range(g * GROUP // ROWS, (g + 1) * GROUP // ROWS):
            lanes = slice(j * ROWS, (j + 1) * ROWS)
            cols = pl.ds(pl.multiple_of((2 * j + h) * ROWS, ROWS), ROWS)
            top, cut = final[h, 0:1, lanes], final[h, 1:2, lanes]
            value = logit[:, cols]
            weighed[:, cols] = jnp.exp(0.5 * (value - top)) * (0.5 + 0.5 * jnp.tanh(value - cut))
            pltpu.make_async_copy(weighed.at[:, cols], out_ref.at[:, cols], out_sem.at[h, j]).start()

    rows_of = [follow(g) for g in range(GROUPS)]
    for _ in range(BISECT_PASSES + 1):
        for part in range(2):
            for rows in rows_of:
                next(rows)
    for rows in rows_of:
        next(rows)
    for g in range(GROUPS):
        weigh(core, g)
    for g in range(GROUPS):
        wait_bytes(final.at[core, :, pl.ds(g * GROUP, GROUP)], final_sem.at[1, g])
        weigh(1 - core, g)
    for rows in rows_of:
        next(rows)
    for rows in rows_of:
        next(rows, None)
    swap = send(scale.at[core], scale.at[core], final_sem.at[0, GROUPS], final_sem.at[1, GROUPS], sibling)
    swap.wait()
    for block in range(8):
        lanes = slice(block // 2 * ROWS, (block // 2 + 1) * ROWS)
        scale_ref[:, block * ROWS : (block + 1) * ROWS] = scale[block % 2, :, lanes]

    for h in range(2):
        for j in range(4):
            cols = pl.ds((2 * j + h) * ROWS, ROWS)
            pltpu.make_async_copy(weighed.at[:, cols], out_ref.at[:, cols], out_sem.at[h, j]).wait()

    def left(m, _):
        cols = pl.ds(0, chunk)
        wait_bytes(xv.at[pl.ds(0, ROWS), cols], c_sem.at[0, m])

        @pl.when(m >= CHUNKS)
        def _():
            wait_bytes(xv.at[pl.ds(0, 32), cols], y_sem.at[0, m])
            wait_bytes(xv.at[pl.ds(0, 64), cols], p_sem.at[0, m])
            wait_bytes(xv.at[pl.ds(0, 32), cols], f_sem.at[0, m])

        return 0

    lax.fori_loop(0, UNITS, left, 0)
    wait_bytes(rowinfo.at[0], row_sem.at[2])
    for j in range(4):
        wait_bytes(half.at[1, :, pl.ds(0, ROWS)], half_sem.at[0, j])
    for g in range(GROUPS):
        wait_bytes(final.at[core, :, pl.ds(g * GROUP, GROUP)], final_sem.at[0, g])
    for (_, in1, _, in2), sems in ((stat_bufs, stat_sem), (mass_bufs, mass_sem), (kept_bufs, kept_sem)):
        for trip in range(in1.shape[0]):
            wait_bytes(in1.at[trip], sems.at[0, trip])
            wait_bytes(in2.at[trip], sems.at[2, trip])


def rescale(weight_ref, scale_ref, out_ref):
    out_ref[...] = weight_ref[...] * scale_ref[...]


def slots(count, height):
    f32 = jnp.float32
    return [
        pltpu.VMEM((count, height, GROUP), f32),
        pltpu.VMEM((count, 15, height, GROUP), f32),
        pltpu.VMEM((count, height, GROUP), f32),
        pltpu.VMEM((count, 3, height, GROUP), f32),
    ]


def on_device(latent_vectors, unembedding_matrix, softmax_divisor, top_probability_quota):
    weights = unembedding_matrix.T
    vocab, depth = weights.shape
    batch = 8 * ROWS
    f32 = jnp.float32
    dma = pltpu.SemaphoreType.DMA
    vmem = pl.BlockSpec(memory_space=pltpu.VMEM)
    hbm = pl.BlockSpec(memory_space=pl.ANY)
    out, scale = pl.pallas_call(
        kernel,
        out_shape=[jax.ShapeDtypeStruct((vocab, batch), f32), jax.ShapeDtypeStruct((1, batch), f32)],
        in_specs=[hbm, hbm, vmem, vmem],
        out_specs=[hbm, vmem],
        scratch_shapes=[
            pltpu.VMEM((batch, depth), jnp.bfloat16),
            pltpu.VMEM((vocab, depth), jnp.bfloat16),
            pltpu.VMEM((vocab, batch), f32),
            pltpu.VMEM((vocab, batch), f32),
            pltpu.VMEM((2, vocab, HALF), f32),
            pltpu.VMEM((2, vocab, HALF), f32),
            pltpu.VMEM((2, 4, 2, ROWS), f32),
            pltpu.VMEM((2, 2, HALF), f32),
            pltpu.VMEM((2, 1, HALF), f32),
            slots(GROUPS, 2),
            slots(GROUPS * BISECT_PASSES, 4),
            slots(GROUPS, 1),
            pltpu.SemaphoreType.REGULAR,
            dma((CHUNKS + 1,)),
            dma((4,)),
            dma((2, UNITS)),
            dma((2, UNITS)),
            dma((2, UNITS)),
            dma((2, UNITS)),
            dma((2, 4)),
            dma((2, GROUPS + 1)),
            dma((2, 4)),
            dma((4, GROUPS)),
            dma((4, GROUPS * BISECT_PASSES)),
            dma((4, GROUPS)),
        ],
        compiler_params=pltpu.CompilerParams(
            collective_id=0, has_side_effects=True, vmem_limit_bytes=58 * 1024 * 1024
        ),
        cost_estimate=pl.CostEstimate(
            flops=2 * vocab * depth * batch, bytes_accessed=2 * depth * (vocab + batch), transcendentals=20 * vocab * batch
        ),
    )(latent_vectors, weights, softmax_divisor[None, :], top_probability_quota[None, :])
    block = pl.BlockSpec((OUT_ROWS, batch), lambda i: (i, 0))
    return pl.pallas_call(
        rescale,
        grid=(pl.cdiv(vocab, OUT_ROWS),),
        out_shape=jax.ShapeDtypeStruct((vocab, batch), f32),
        in_specs=[block, pl.BlockSpec((1, batch), lambda i: (0, 0))],
        out_specs=block,
    )(out, scale).T


def solution(mesh):
    placed = (P("dp", None), P(None, ("dp", "vocab")), P("dp"), P("dp"))
    return jax.shard_map(
        on_device, mesh=mesh, in_specs=placed, out_specs=P(None, ("dp", "vocab")), check_vma=False
    )
```
